32 devices in a mesh: grp: 4 (over y, x), vid: 8 (over z, core).
Axes of the slice: x: 2, y: 2, z: 4, core: 2. Of those that a mesh axis runs over, the one named last changes fastest.
Arguments:
- frames: bfloat16 [32768, 1024], P(('grp', 'vid')), parts along dimension 0, may hold values from -240 to 240
- w_frame: bfloat16 [1024, 512], replicated, may hold values from -0.1875 to 0.1875
- step_emb: bfloat16 [4096, 512], P(('grp', 'vid')), parts along dimension 0, may hold values from -6 to 6
- targets: int32 [32768], P(('grp', 'vid')), parts along dimension 0, may hold values from 0 to 127
- tile_frame: int32 [32, 64], P(('grp', 'vid')), parts along dimension 0, may hold values from 0 to 7, as said below
- tile_step: int32 [32, 64], P(('grp', 'vid')), parts along dimension 0, may hold values from 0 to 7, as said below
- tile_count: int32 [32], P(('grp', 'vid')), parts along dimension 0, may hold values from 8 to 64, as said below
Outputs:
- row_loss: float32 [32768], P(('grp', 'vid')), parts along dimension 0
- frame_grad: bfloat16 [32768, 1024], P(('grp', 'vid')), parts along dimension 0
- step_grad: float32 [4096, 512], P(('grp', 'vid')), parts along dimension 0
The draws below stay inside these ranges and needn't reach their ends.
There are 4 independent parts, one for each index of `grp`. The reference program is written for one: setup_inputs(seed, part) draws one part's arguments, and reference() takes and returns one part's arrays. A program takes and returns all parts, laid end to end along the dimension named above; an argument that names none is the same for every part. Nothing has to cross between parts.
Inputs may be any that keep to these rules, and one draw needn't show every extreme that they name: `tile_frame`: each run of 8 tiles of a list, starting at a multiple of 8, names every frame block once. `tile_step`: the (frame block, step block) pairs of one video's list are distinct; the first 8 tiles pair each frame block with the video's own step block. Only the first tile_count tiles of a list are valid; some video's list is full.
All inputs are finite; a program needn't handle non-finite values.
Results may differ from the reference program's by a relative error of at most 0.0086.
Values may be sent and summed in bfloat16 or wider, within the bound.
No kernel may reach another device: no remote copies, remote signals or barrier semaphores. Data moves between devices by JAX's collectives and lax.ppermute only.
A program may use at most 128 MiB of HBM per device.

```python
import math
import jax
import jax.numpy as jnp
from jax import lax

D = 1024
E = 512
S_DEV = 128
FR_DEV = 1024
MAXT = 64
FRAMES = 8192
STEPS = 1024
N_VID = 8


def draw_frames(key, part):
    first = jax.random.fold_in(key, 0)
    base = jax.random.normal(first, (FRAMES, D), jnp.float32)
    return jnp.clip(base, -240.0, 240.0).astype(jnp.bfloat16)


def tile_tables(key):
    inner = jax.random.fold_in(key, 7)
    count_key, perm_key, pick_key, order_key = jax.random.split(inner, 4)
    blocks = FR_DEV // 128
    rounds = MAXT // blocks
    keys = jax.random.split(perm_key, N_VID)
    perms = jax.vmap(lambda single: jax.random.permutation(single, N_VID - 1))(keys)
    order_keys = jax.random.split(order_key, N_VID * rounds)
    orders = jax.vmap(lambda single: jax.random.permutation(single, blocks))(order_keys)
    frame_tab = orders.reshape(N_VID, MAXT).astype(jnp.int32)
    slots = jnp.arange(MAXT, dtype=jnp.int32)
    round_of = slots // blocks
    column = (round_of[None, :] - 1 + frame_tab) % (N_VID - 1)
    videos = jnp.arange(N_VID, dtype=jnp.int32)[:, None]
    other = (videos + 1 + jnp.take_along_axis(perms, column, axis=1)) % N_VID
    step_of = jnp.where(round_of[None, :] == 0, videos, other).astype(jnp.int32)
    counts = jax.random.randint(count_key, (N_VID,), blocks, MAXT + 1)
    chosen = jax.random.randint(pick_key, (), 0, N_VID)
    counts = jnp.where(jnp.arange(N_VID) == chosen, MAXT, counts).astype(jnp.int32)
    return (frame_tab, step_of, counts)


def draw_tile_frame(key, part):
    return tile_tables(key)[0]


def draw_tile_step(key, part):
    return tile_tables(key)[1]


def draw_tile_count(key, part):
    return tile_tables(key)[2]


def with_ends(result, stream_key, least, top_value):
    spot = [jax.random.randint(jax.random.fold_in(stream_key, axis), (), 0, length) for axis, length in enumerate(result.shape)]
    widest = result.shape.index(max(result.shape))
    beside = spot[:widest] + [(spot[widest] + 1) % result.shape[widest]] + spot[widest + 1:]
    return result.at[tuple(spot)].set(least).at[tuple(beside)].set(top_value)


def steps_of(stream_key, dims, cuts, smallest, largest):
    level = 1.0
    for dim, parts in cuts:
        steps = jax.random.uniform(jax.random.fold_in(jax.random.fold_in(stream_key, 6), dim), (parts,), jnp.float32, smallest / len(cuts), largest / len(cuts))
        level = level * jnp.repeat(jnp.exp(steps), dims[dim] // parts).reshape((-1,) + (1,) * (len(dims) - 1 - dim))
    return level


def noise(rng, extent, deviation, limit, shards=(), kind=jnp.bfloat16):
    values = jax.random.normal(rng, extent, jnp.float32) * deviation
    if len(shards) > 0:
        values = steps_of(rng, extent, shards, -0.22, 0.18) * values
    return jnp.clip(values, min=-limit, max=limit).astype(kind)


def setup_inputs(seed: int = 0, part: int = 0) -> dict:
    seeds = jax.random.split(jax.random.key(seed), 8)
    part_keys = jax.random.split(jax.random.fold_in(seeds[7], part), 8)
    frames = draw_frames(jax.random.fold_in(jax.random.fold_in(seeds[7], part), 71), part)
    w_frame = noise(seeds[1], (D, E), D ** -0.5, 0.1875)
    step_emb = noise(part_keys[2], (STEPS, E), 1.0, 6.0, ((0, 8),))
    targets = with_ends(jax.random.randint(part_keys[3], (FRAMES,), 0, S_DEV), jax.random.fold_in(part_keys[3], 1), 0, S_DEV - 1).astype(jnp.int32)
    tile_frame = draw_tile_frame(jax.random.fold_in(jax.random.fold_in(seeds[7], part), 71), part)
    tile_step = draw_tile_step(jax.random.fold_in(jax.random.fold_in(seeds[7], part), 71), part)
    tile_count = draw_tile_count(jax.random.fold_in(jax.random.fold_in(seeds[7], part), 71), part)
    return dict(frames=frames, w_frame=w_frame, step_emb=step_emb, targets=targets, tile_frame=tile_frame, tile_step=tile_step, tile_count=tile_count)


def reference(frames, w_frame, step_emb, targets, tile_frame, tile_step, tile_count):
    width = step_emb.shape[1]
    temper = 1.0 / math.sqrt(width)
    blocks = FR_DEV // 128

    def per_video(carry, video):
        video = video.astype(jnp.int32)
        rows_v = lax.dynamic_slice_in_dim(frames, video * FR_DEV, FR_DEV)
        goals = lax.dynamic_slice_in_dim(targets, video * FR_DEV, FR_DEV)
        embedded = jnp.dot(rows_v, w_frame, preferred_element_type=jnp.float32).astype(jnp.bfloat16)
        valid = (jnp.arange(MAXT) < tile_count[video]).astype(jnp.int32)
        allowed = jnp.zeros((blocks, N_VID), jnp.int32).at[tile_frame[video], tile_step[video]].max(valid)
        wide = jnp.repeat(jnp.repeat(allowed, 128, axis=0), S_DEV, axis=1) > 0
        scores = jnp.dot(embedded, step_emb.T, preferred_element_type=jnp.float32) * temper
        top = lax.optimization_barrier(jnp.max(jnp.where(wide, scores, -jnp.inf), axis=1, keepdims=True))
        total = lax.optimization_barrier(jnp.sum(jnp.where(wide, jnp.exp(jnp.where(wide, scores - top, 0.0)), 0.0), axis=1, keepdims=True))
        lse = top + jnp.log(total)
        owners = (video * S_DEV + goals).astype(jnp.int32)
        chosen = step_emb[owners].astype(jnp.float32)
        positive = lax.optimization_barrier(jnp.sum(embedded.astype(jnp.float32) * chosen, axis=1)) * temper
        loss = lse[:, 0] - positive
        probs = jnp.where(wide, jnp.exp(jnp.where(wide, scores - lse, 0.0)), 0.0).astype(jnp.bfloat16)
        grad_rows = jnp.dot(probs, step_emb, preferred_element_type=jnp.float32) * temper - chosen * temper
        frame_grad = lax.dot_general(grad_rows.astype(jnp.bfloat16), w_frame, (((1,), (1,)), ((), ())), preferred_element_type=jnp.float32).astype(jnp.bfloat16)
        grad_cols = jnp.dot(probs.T, embedded, preferred_element_type=jnp.float32) * temper
        own_term = jax.ops.segment_sum(embedded.astype(jnp.float32) * temper, owners, num_segments=N_VID * S_DEV)
        return (carry + grad_cols - own_term, (loss, frame_grad))
    start = jnp.zeros((N_VID * S_DEV, width), jnp.float32)
    step_grad, (losses, grads) = lax.scan(per_video, start, jnp.arange(N_VID, dtype=jnp.int32))
    return (losses.reshape(-1), grads.reshape(-1, frames.shape[1]), step_grad)
```

```python
import math

import jax
import jax.numpy as jnp
from jax import lax
from jax.experimental import pallas as pl
from jax.experimental.pallas import tpu as pltpu
from jax.sharding import PartitionSpec as P

F32 = jnp.float32
BF16 = jnp.bfloat16
HIDDEN = -1e30
NT = (((1,), (1,)), ((), ()))
TN = (((0,), (0,)), ((), ()))
VMEM = pl.BlockSpec(memory_space=pltpu.VMEM)
SMEM = pl.BlockSpec(memory_space=pltpu.SMEM)


def params(mib):
    return pltpu.CompilerParams(vmem_limit_bytes=mib * 2**20)


def cost(flops, nbytes, exps=0):
    return pl.CostEstimate(flops=flops, bytes_accessed=nbytes, transcendentals=exps)


def embed_kernel(where_ref, count_ref, tf_ref, ts_ref, x_ref, w_ref, e_ref, bias_ref):
    e_ref[...] = jnp.dot(x_ref[...], w_ref[...], preferred_element_type=F32).astype(BF16)

    @pl.when(pl.program_id(0) == 0)
    def _():
        chips = bias_ref.shape[0] // 2
        rows = bias_ref.shape[1]
        slots = tf_ref.shape[1]
        z, core = where_ref[0] >> 1, where_ref[0] & 1
        line = lax.broadcasted_iota(jnp.int32, (2 * chips, slots), 0)
        place = lax.broadcasted_iota(jnp.int32, (2 * chips, slots), 1)
        back = z - (line >> 1)
        video = 2 * jnp.where(back < 0, back + chips, back)
        second = line & 1
        video = video + jnp.where(core == 0, second, 1 - second)
        left = jnp.where((ts_ref[...] == video) & (place < count_ref[0]), 1.0, 0.0)
        block = lax.broadcasted_iota(jnp.int32, (rows, slots), 0) // 128
        right = jnp.where(tf_ref[...] == block, 1.0, 0.0)
        seen = lax.dot_general(left.astype(BF16), right.astype(BF16), NT, preferred_element_type=F32)
        bias_ref[...] = jnp.where(seen > 0.5, 0.0, HIDDEN)


def embed(where, count, tile_frame, tile_step, frames, w, videos):
    rows, depth = frames.shape
    width = w.shape[1]
    tile = rows // 4
    return pl.pallas_call(
        embed_kernel,
        grid=(rows // tile,),
        in_specs=[
            SMEM,
            SMEM,
            VMEM,
            VMEM,
            pl.BlockSpec((tile, depth), lambda i: (i, 0)),
            pl.BlockSpec((depth, width), lambda i: (0, 0)),
        ],
        out_specs=[
            pl.BlockSpec((tile, width), lambda i: (i, 0)),
            pl.BlockSpec((videos, rows), lambda i: (0, 0)),
        ],
        out_shape=[
            jax.ShapeDtypeStruct((rows, width), BF16),
            jax.ShapeDtypeStruct((videos, rows), F32),
        ],
        cost_estimate=cost(2 * rows * depth * width, 2 * (rows * depth + depth * width + rows * width)),
        compiler_params=params(32),
        name="embed",
    )(where, count, tile_frame, tile_step, frames, w)


def middle_kernel(chips, temper, *refs):
    n = 2 * chips
    e_ref, bias_ref, goal_ref = refs[:3]
    blocks = refs[3 : 3 + n]
    loss_ref, q_ref = refs[3 + n : 5 + n]
    outs = refs[5 + n : 5 + 2 * n]
    s_ref = refs[5 + 2 * n]
    rows = e_ref.shape[0]
    own = blocks[0].shape[0]
    tile = s_ref.shape[1]

    def columns(turn, carry):
        at = pl.ds(pl.multiple_of(turn * tile, tile), tile)
        e = e_ref[at, :]
        top = None
        hit = goal_ref[:, at] == lax.broadcasted_iota(jnp.int32, (own, tile), 0)
        pos = None
        for b in range(n):
            s = lax.dot_general(blocks[b][...], e, NT, preferred_element_type=F32) * temper
            if b == 0:
                pos = jnp.sum(jnp.where(hit, s, 0.0), axis=0, keepdims=True)
            s = s + bias_ref[b : b + 1, at]
            s_ref[b * own : (b + 1) * own, :] = s
            high = jnp.max(s, axis=0, keepdims=True)
            top = high if b == 0 else jnp.maximum(top, high)
        total = None
        for b in range(n):
            p = jnp.exp(s_ref[b * own : (b + 1) * own, :] - top)
            s_ref[b * own : (b + 1) * own, :] = p
            part = jnp.sum(p, axis=0, keepdims=True)
            total = part if b == 0 else total + part
        loss_ref[:, at] = top + jnp.log(total) - pos
        scale = 1.0 / total
        for b in range(n):
            q = (s_ref[b * own : (b + 1) * own, :] * scale).astype(BF16)
            if b == 0:
                q = (q.astype(F32) - jnp.where(hit, 1.0, 0.0)).astype(BF16)
            q_ref[b * own : (b + 1) * own, at] = q
        return carry

    lax.fori_loop(0, rows // tile, columns, 0)
    for b in range(n):
        out = jnp.dot(
            q_ref[b * own : (b + 1) * own, :], e_ref[...], preferred_element_type=F32
        )
        outs[b][...] = out.astype(outs[b].dtype)


def middle(e, bias, goals, blocks, temper):
    n = len(blocks)
    rows, width = e.shape
    own = blocks[0].shape[0]
    return pl.pallas_call(
        lambda *refs: middle_kernel(n // 2, temper, *refs),
        in_specs=[VMEM] * (3 + n),
        out_specs=[VMEM] * (2 + n),
        out_shape=[
            jax.ShapeDtypeStruct((1, rows), F32),
            jax.ShapeDtypeStruct((n * own, rows), BF16),
        ]
        + [jax.ShapeDtypeStruct((own, width), F32 if b % 2 == 0 else BF16) for b in range(n)],
        scratch_shapes=[pltpu.VMEM((n * own, 256), F32)],
        cost_estimate=cost(
            4 * n * own * rows * width,
            2 * rows * width + 6 * n * own * width + 2 * n * own * rows,
            n * own * rows,
        ),
        compiler_params=params(48),
        name="middle",
    )(e, bias, goals, *blocks)


def back_kernel(temper, *refs):
    n = len(refs) - 4
    q_ref, w_ref = refs[:2]
    blocks = refs[2 : 2 + n]
    out_ref, table_ref = refs[2 + n :]
    own = blocks[0].shape[0]

    @pl.when(pl.program_id(0) == 0)
    def _():
        for b in range(n):
            table_ref[b * own : (b + 1) * own, :] = blocks[b][...]

    rows = lax.dot_general(q_ref[...], table_ref[...], TN, preferred_element_type=F32) * temper
    out_ref[...] = lax.dot_general(
        rows.astype(BF16), w_ref[...], NT, preferred_element_type=F32
    ).astype(BF16)


def back(q, w, blocks, temper):
    n = len(blocks)
    steps, rows = q.shape
    depth, width = w.shape
    own = blocks[0].shape[0]
    tile = rows // 4
    return pl.pallas_call(
        lambda *refs: back_kernel(temper, *refs),
        grid=(rows // tile,),
        in_specs=[
            pl.BlockSpec((steps, tile), lambda i: (0, i)),
            pl.BlockSpec((depth, width), lambda i: (0, 0)),
        ]
        + [pl.BlockSpec((own, width), lambda i: (0, 0))] * n,
        out_specs=pl.BlockSpec((tile, depth), lambda i: (i, 0)),
        out_shape=jax.ShapeDtypeStruct((rows, depth), BF16),
        scratch_shapes=[pltpu.VMEM((steps, width), BF16)],
        cost_estimate=cost(
            2 * rows * width * (steps + depth),
            2 * (steps * rows + depth * width + steps * width + rows * depth),
        ),
        compiler_params=params(40),
        name="back",
    )(q, w, *blocks)


def shards(frames, w_frame, step_emb, targets, tile_frame, tile_step, tile_count):
    videos = lax.axis_size("vid")
    chips = videos // 2
    temper = 1.0 / math.sqrt(step_emb.shape[1])
    place = lax.axis_index("vid").astype(jnp.int32)
    swap = [(i, i ^ 1) for i in range(videos)]

    def along(k):
        return [(i, (i // 2 + k) % chips * 2 + i % 2) for i in range(videos)]

    mine = [step_emb] + [lax.ppermute(step_emb, "vid", along(k)) for k in range(1, chips)]
    theirs = [lax.ppermute(block, "vid", swap) for block in mine]
    blocks = [block for pair in zip(mine, theirs) for block in pair]
    e, bias = embed(place.reshape(1), tile_count, tile_frame, tile_step, frames, w_frame, videos)
    loss, q, *parts = middle(e, bias, targets.reshape(1, -1), blocks, temper)
    total = None
    for k in range(chips - 1, -1, -1):
        whole = parts[2 * k] + lax.ppermute(parts[2 * k + 1], "vid", swap).astype(F32)
        if k > 0:
            whole = lax.ppermute(whole.astype(BF16), "vid", along(chips - k)).astype(F32)
        total = whole if total is None else total + whole
    frame_grad = back(q, w_frame, blocks, temper)
    return (loss.reshape(-1), frame_grad, total * temper)


def solution(mesh):
    placed = (
        P(("grp", "vid"), None),
        P(),
        P(("grp", "vid"), None),
        P(("grp", "vid")),
        P(("grp", "vid"), None),
        P(("grp", "vid"), None),
        P(("grp", "vid")),
    )
    return jax.shard_map(
        shards,
        mesh=mesh,
        in_specs=placed,
        out_specs=(P(("grp", "vid")), P(("grp", "vid"), None), P(("grp", "vid"), None)),
        check_vma=False,
    )
```

```python
import math

import jax
import jax.numpy as jnp
from jax import lax
from jax.experimental import pallas as pl
from jax.experimental.pallas import tpu as pltpu
from jax.sharding import PartitionSpec as P

F32 = jnp.float32
BF16 = jnp.bfloat16
HIDDEN = -1e30
EMBED_MIB = 52
NT = (((1,), (1,)), ((), ()))
TN = (((0,), (0,)), ((), ()))
VMEM = pl.BlockSpec(memory_space=pltpu.VMEM)
SMEM = pl.BlockSpec(memory_space=pltpu.SMEM)


def params(mib):
    return pltpu.CompilerParams(vmem_limit_bytes=mib * 2**20)


def cost(flops, nbytes, exps=0):
    return pl.CostEstimate(flops=flops, bytes_accessed=nbytes, transcendentals=exps)


def embed_kernel(x_ref, w_ref, e_ref):
    e_ref[...] = jnp.dot(x_ref[...], w_ref[...], preferred_element_type=F32).astype(BF16)


def embed(frames, w):
    rows, depth = frames.shape
    width = w.shape[1]
    tile = rows // 4
    return pl.pallas_call(
        embed_kernel,
        grid=(rows // tile,),
        in_specs=[
            pl.BlockSpec((tile, depth), lambda i: (i, 0)),
            pl.BlockSpec((depth, width), lambda i: (0, 0)),
        ],
        out_specs=pl.BlockSpec((tile, width), lambda i: (i, 0)),
        out_shape=jax.ShapeDtypeStruct((rows, width), BF16),
        cost_estimate=cost(2 * rows * depth * width, 2 * (rows * depth + depth * width + rows * width)),
        compiler_params=params(EMBED_MIB),
        name="embed",
    )(frames, w)


def sight(place, count, tf, ts, shape):
    videos, rows = shape
    chips = videos // 2
    slots = tf.shape[1]
    line = lax.broadcasted_iota(jnp.int32, (videos, slots), 0)
    slot = lax.broadcasted_iota(jnp.int32, (videos, slots), 1)
    back = (place >> 1) - (line >> 1)
    second = line & 1
    video = 2 * jnp.where(back < 0, back + chips, back)
    video = video + jnp.where((place & 1) == 0, second, 1 - second)
    left = jnp.where((ts == video) & (slot < count), 1.0, 0.0)
    block = lax.broadcasted_iota(jnp.int32, (rows, slots), 0) // 128
    right = jnp.where(tf == block, 1.0, 0.0)
    seen = lax.dot_general(left.astype(BF16), right.astype(BF16), NT, preferred_element_type=F32)
    return jnp.where(seen > 0.5, 0.0, HIDDEN)


def stack(refs):
    values = [ref[...] for ref in refs]
    return values[0] if len(values) == 1 else jnp.concatenate(values, axis=0)


def tiles(rows):
    return [slice(at, at + 256) for at in range(0, rows, 256)]


def score_kernel(k, parts, temper, *refs):
    e_ref = refs[0]
    blocks = refs[1 : 1 + parts]
    if k == 0:
        place_ref, count_ref, tf_ref, ts_ref, goal_ref = refs[1 + parts : 6 + parts]
        p_ref, top_ref, total_ref, pos_ref, bias_ref = refs[6 + parts :]
        bias_ref[...] = sight(place_ref[0], count_ref[0], tf_ref[...], ts_ref[...], bias_ref.shape)
    else:
        bias_ref, top_in, total_in, p_ref, top_ref, total_ref = refs[1 + parts :]
    chunk = stack(blocks)
    steps = chunk.shape[0]
    own = steps // 2
    for at in tiles(e_ref.shape[0]):
        s = lax.dot_general(chunk, e_ref[at, :], NT, preferred_element_type=F32) * temper
        bias = bias_ref[2 * k : 2 * k + 2, at]
        first, second = s[:own] + bias[0:1], s[own:] + bias[1:2]
        top = jnp.maximum(
            jnp.max(first, axis=0, keepdims=True), jnp.max(second, axis=0, keepdims=True)
        )
        if k == 0:
            hit = goal_ref[:, at] == lax.broadcasted_iota(jnp.int32, first.shape, 0)
            pos_ref[:, at] = jnp.sum(jnp.where(hit, s[:own], 0.0), axis=0, keepdims=True)
        else:
            top = jnp.maximum(top, top_in[:, at])
        first, second = jnp.exp(first - top), jnp.exp(second - top)
        p_ref[:own, at] = first
        p_ref[own:, at] = second
        total = jnp.sum(first, axis=0, keepdims=True) + jnp.sum(second, axis=0, keepdims=True)
        if k > 0:
            total = total + total_in[:, at] * jnp.exp(top_in[:, at] - top)
        top_ref[:, at] = top
        total_ref[:, at] = total


def score(k, videos, temper, e, chunk, *more):
    rows, width = e.shape
    steps = sum(part.shape[0] for part in chunk)
    line = jax.ShapeDtypeStruct((1, rows), F32)
    extra = [line, jax.ShapeDtypeStruct((videos, rows), F32)] if k == 0 else []
    specs = [SMEM, SMEM, VMEM, VMEM, VMEM] if k == 0 else [VMEM] * len(more)
    return pl.pallas_call(
        lambda *refs: score_kernel(k, len(chunk), temper, *refs),
        in_specs=[VMEM] * (1 + len(chunk)) + specs,
        out_specs=[VMEM] * (3 + len(extra)),
        out_shape=[jax.ShapeDtypeStruct((steps, rows), F32), line, line] + extra,
        cost_estimate=cost(
            2 * steps * rows * width, 2 * (rows + steps) * width + 4 * steps * rows, steps * rows
        ),
        compiler_params=params(24),
        name=f"score_{k}",
    )(e, *chunk, *more)


def share_kernel(k, *refs):
    p_ref, top_ref, last_ref, total_ref, e_ref = refs[:5]
    if k == 0:
        goal_ref, pos_ref, q_ref, mine_ref, other_ref, loss_ref = refs[5:]
        loss_ref[...] = last_ref[...] + jnp.log(total_ref[...]) - pos_ref[...]
    else:
        q_ref, mine_ref, other_ref = refs[5:]
    own = mine_ref.shape[0]
    scale = jnp.exp(top_ref[...] - last_ref[...]) / total_ref[...]
    out = None
    for at in tiles(e_ref.shape[0]):
        q = (p_ref[:, at] * scale[:, at]).astype(BF16)
        if k == 0:
            hit = goal_ref[:, at] == lax.broadcasted_iota(jnp.int32, q.shape, 0)
            q = (q.astype(F32) - jnp.where(hit, 1.0, 0.0)).astype(BF16)
        q_ref[:, at] = q
        part = jnp.dot(q, e_ref[at, :], preferred_element_type=F32)
        out = part if out is None else out + part
    mine_ref[...] = out[:own]
    other_ref[...] = out[own:].astype(BF16)


def share(k, p, top, last, total, e, *more):
    steps, rows = p.shape
    width = e.shape[1]
    own = steps // 2
    return pl.pallas_call(
        lambda *refs: share_kernel(k, *refs),
        in_specs=[VMEM] * (5 + len(more)),
        out_specs=[VMEM] * (4 if k == 0 else 3),
        out_shape=[
            jax.ShapeDtypeStruct((steps, rows), BF16),
            jax.ShapeDtypeStruct((own, width), F32),
            jax.ShapeDtypeStruct((own, width), BF16),
        ]
        + [jax.ShapeDtypeStruct((1, rows), F32)] * (k == 0),
        cost_estimate=cost(2 * steps * rows * width, 6 * steps * rows + 2 * rows * width),
        compiler_params=params(24),
        name=f"share_{k}",
    )(p, top, last, total, e, *more)


def back_kernel(sizes, temper, *refs):
    n = len(sizes)
    w_ref, out_ref = refs[0], refs[-1]
    rows = None
    at = 1 + n
    for k in range(n):
        chunk = stack(refs[at : at + sizes[k]])
        at += sizes[k]
        part = lax.dot_general(refs[1 + k][...], chunk, TN, preferred_element_type=F32)
        rows = part if rows is None else rows + part
    out_ref[...] = lax.dot_general(
        (rows * temper).astype(BF16), w_ref[...], NT, preferred_element_type=F32
    ).astype(BF16)


def back(w, qs, chunks, temper):
    n = len(qs)
    steps, rows = qs[0].shape
    depth, width = w.shape
    tile = rows // 4
    flat = [part for chunk in chunks for part in chunk]
    return pl.pallas_call(
        lambda *refs: back_kernel([len(chunk) for chunk in chunks], temper, *refs),
        grid=(rows // tile,),
        in_specs=[pl.BlockSpec((depth, width), lambda i: (0, 0))]
        + [pl.BlockSpec((steps, tile), lambda i: (0, i))] * n
        + [pl.BlockSpec(part.shape, lambda i: (0, 0)) for part in flat],
        out_specs=pl.BlockSpec((tile, depth), lambda i: (i, 0)),
        out_shape=jax.ShapeDtypeStruct((rows, depth), BF16),
        cost_estimate=cost(
            2 * rows * width * (n * steps + depth),
            2 * (n * steps * (rows + width) + depth * width + rows * depth),
        ),
        compiler_params=params(40),
        name="back",
    )(w, *qs, *flat)


def shards(frames, w_frame, step_emb, targets, tile_frame, tile_step, tile_count):
    videos = lax.axis_size("vid")
    chips = videos // 2
    far = chips // 2
    own, width = step_emb.shape
    half = own // 2
    temper = 1.0 / math.sqrt(width)
    place = lax.axis_index("vid").astype(jnp.int32)

    def along(x, k):
        pairs = [(i, (i // 2 + k) % chips * 2 + i % 2) for i in range(videos)]
        return lax.ppermute(x, "vid", pairs)

    def swap(x):
        return lax.ppermute(x, "vid", [(i, i ^ 1) for i in range(videos)])

    goals = targets.reshape(1, -1)
    e = embed(frames, w_frame)
    found = swap(step_emb)

    mine = {0: [step_emb]}
    right = left = step_emb
    for k in range(1, far):
        right, left = along(right, 1), along(left, -1)
        if k == 1:
            right, left, e = lax.optimization_barrier((right, left, e))
        mine[k], mine[chips - k] = [right], [left]
    mine[far] = [along(right[:half], 1), along(left[half:], -1)]

    order = [0] + [c for k in range(1, far) for c in (k, chips - k)] + [far]
    chunks, kept = {}, {}
    more = (place.reshape(1), tile_count, tile_frame, tile_step, goals)
    for k in order:
        if k == far and far > 1:
            (*mine[k], top) = lax.optimization_barrier((*mine[k], top))
        chunks[k] = mine[k] + ([found] if k == 0 else [swap(part) for part in mine[k]])
        p, top, total, *first = score(k, videos, temper, e, chunks[k], *more)
        kept[k] = (p, top)
        if k == 0:
            pos, bias = first
        more = (bias, top, total)
    last = top

    qs, whole = {}, {}
    for n, k in enumerate(reversed(order)):
        if n == 2:
            e, whole[far] = lax.optimization_barrier((e, whole[far]))
        if k == 0:
            e, qs[1] = lax.optimization_barrier((e, qs[1]))
        more = (goals, pos) if k == 0 else ()
        qs[k], part, other, *loss = share(k, *kept[k], last, total, e, *more)
        whole[k] = part + swap(other).astype(F32)
    right = along(whole[far][:half].astype(BF16), 1).astype(F32)
    left = along(whole[far][half:].astype(BF16), -1).astype(F32)
    for k in range(far - 1, 0, -1):
        up, down = whole[chips - k], whole[k]
        if k == far - 1:
            up = jnp.concatenate([up[:half] + right, up[half:]], axis=0)
            down = jnp.concatenate([down[:half], down[half:] + left], axis=0)
        else:
            up, down = up + right, down + left
        right = along(up.astype(BF16), 1).astype(F32)
        left = along(down.astype(BF16), -1).astype(F32)
    step_grad = (whole[0] + right + left) * temper
    frame_grad = back(
        w_frame, [qs[k] for k in order], [chunks[k] for k in order], temper
    )
    return (loss[0].reshape(-1), frame_grad, step_grad)


def solution(mesh):
    placed = (
        P(("grp", "vid"), None),
        P(),
        P(("grp", "vid"), None),
        P(("grp", "vid")),
        P(("grp", "vid"), None),
        P(("grp", "vid"), None),
        P(("grp", "vid")),
    )
    return jax.shard_map(
        shards,
        mesh=mesh,
        in_specs=placed,
        out_specs=(P(("grp", "vid")), P(("grp", "vid"), None), P(("grp", "vid"), None)),
        check_vma=False,
    )
```

```python
import math

import jax
import jax.numpy as jnp
from jax import lax
from jax.experimental import pallas as pl
from jax.experimental.pallas import tpu as pltpu
from jax.sharding import PartitionSpec as P

F32 = jnp.float32
BF16 = jnp.bfloat16
HIDDEN = -1e30
EMBED_MIB = 52
TILES = 4
NT = (((1,), (1,)), ((), ()))
TN = (((0,), (0,)), ((), ()))
VMEM = pl.BlockSpec(memory_space=pltpu.VMEM)
SMEM = pl.BlockSpec(memory_space=pltpu.SMEM)


def params(mib):
    return pltpu.CompilerParams(vmem_limit_bytes=mib * 2**20)


def cost(flops, nbytes, exps=0, scale=1):
    return pl.CostEstimate(
        flops=flops // scale, bytes_accessed=nbytes // scale, transcendentals=exps // scale
    )


def embed_kernel(x_hbm, w_hbm, e_ref, x_ref, w_ref, sem):
    tile = x_ref.shape[0] // TILES
    deep = w_ref.shape[0] // TILES
    reads = []
    for n in range(TILES):
        at = pl.ds(n * deep, deep)
        reads.append(pltpu.make_async_copy(w_hbm.at[at], w_ref.at[at], sem.at[n]))
    for n in range(TILES):
        at = pl.ds(n * tile, tile)
        reads.append(pltpu.make_async_copy(x_hbm.at[at], x_ref.at[at], sem.at[TILES + n]))
    for read in reads:
        read.start()
    for read in reads[:TILES]:
        read.wait()
    for n in range(TILES):
        reads[TILES + n].wait()
        at = slice(n * tile, (n + 1) * tile)
        e_ref[at, :] = jnp.dot(x_ref[at, :], w_ref[...], preferred_element_type=F32).astype(BF16)


def embed(frames, w):
    rows, depth = frames.shape
    width = w.shape[1]
    return pl.pallas_call(
        embed_kernel,
        in_specs=[pl.BlockSpec(memory_space=pl.ANY)] * 2,
        out_specs=VMEM,
        out_shape=jax.ShapeDtypeStruct((rows, width), BF16),
        scratch_shapes=[
            pltpu.VMEM((rows, depth), BF16),
            pltpu.VMEM((depth, width), BF16),
            pltpu.SemaphoreType.DMA((2 * TILES,)),
        ],
        cost_estimate=cost(2 * rows * depth * width, 2 * (rows * depth + depth * width + rows * width)),
        compiler_params=params(EMBED_MIB),
        name="embed",
    )(frames, w)


def sight(place, count, tf, ts, shape):
    videos, rows = shape
    slots = tf.shape[1]
    line = lax.broadcasted_iota(jnp.int32, (videos, slots), 0)
    slot = lax.broadcasted_iota(jnp.int32, (videos, slots), 1)
    video = line ^ place
    left = jnp.where((ts == video) & (slot < count), 1.0, 0.0)
    block = lax.broadcasted_iota(jnp.int32, (rows, slots), 0) // 128
    right = jnp.where(tf == block, 1.0, 0.0)
    seen = lax.dot_general(left.astype(BF16), right.astype(BF16), NT, preferred_element_type=F32)
    return jnp.where(seen > 0.5, 0.0, HIDDEN)


def stack(refs):
    values = [ref[...] for ref in refs]
    return values[0] if len(values) == 1 else jnp.concatenate(values, axis=0)


def tiles(rows):
    return [slice(at, at + 256) for at in range(0, rows, 256)]


def score_kernel(k, parts, temper, *refs):
    e_ref = refs[0]
    blocks = refs[1 : 1 + parts]
    if k == 0:
        place_ref, count_ref, tf_ref, ts_ref, goal_ref = refs[1 + parts : 6 + parts]
        p_ref, top_ref, total_ref, pos_ref, bias_ref = refs[6 + parts :]
        bias_ref[...] = sight(place_ref[0], count_ref[0], tf_ref[...], ts_ref[...], bias_ref.shape)
    else:
        bias_ref, top_in, total_in, p_ref, top_ref, total_ref = refs[1 + parts :]
    chunk = stack(blocks)
    steps = chunk.shape[0]
    own = steps // 2
    for at in tiles(e_ref.shape[0]):
        s = lax.dot_general(chunk, e_ref[at, :], NT, preferred_element_type=F32) * temper
        bias = bias_ref[2 * k : 2 * k + 2, at]
        first, second = s[:own] + bias[0:1], s[own:] + bias[1:2]
        top = jnp.maximum(
            jnp.max(first, axis=0, keepdims=True), jnp.max(second, axis=0, keepdims=True)
        )
        if k == 0:
            hit = goal_ref[:, at] == lax.broadcasted_iota(jnp.int32, first.shape, 0)
            pos_ref[:, at] = jnp.sum(jnp.where(hit, s[:own], 0.0), axis=0, keepdims=True)
        else:
            top = jnp.maximum(top, top_in[:, at])
        first, second = jnp.exp(first - top), jnp.exp(second - top)
        p_ref[:own, at] = first
        p_ref[own:, at] = second
        total = jnp.sum(first, axis=0, keepdims=True) + jnp.sum(second, axis=0, keepdims=True)
        if k > 0:
            total = total + total_in[:, at] * jnp.exp(top_in[:, at] - top)
        top_ref[:, at] = top
        total_ref[:, at] = total


def score(k, videos, temper, e, chunk, *more):
    rows, width = e.shape
    steps = sum(part.shape[0] for part in chunk)
    line = jax.ShapeDtypeStruct((1, rows), F32)
    extra = [line, jax.ShapeDtypeStruct((videos, rows), F32)] if k == 0 else []
    specs = [SMEM, SMEM, VMEM, VMEM, VMEM] if k == 0 else [VMEM] * len(more)
    return pl.pallas_call(
        lambda *refs: score_kernel(k, len(chunk), temper, *refs),
        in_specs=[VMEM] * (1 + len(chunk)) + specs,
        out_specs=[VMEM] * (3 + len(extra)),
        out_shape=[jax.ShapeDtypeStruct((steps, rows), F32), line, line] + extra,
        cost_estimate=cost(
            2 * steps * rows * width, 2 * (rows + steps) * width + 4 * steps * rows, steps * rows
        ),
        compiler_params=params(24),
        name=f"score_{k}",
    )(e, *chunk, *more)


def share_kernel(ks, *refs):
    last_ref, total_ref, e_ref = refs[:3]
    ins, outs = refs[3 : 3 + 2 * len(ks)], refs[3 + 2 * len(ks) :]
    if 0 in ks:
        goal_ref, pos_ref = outs[:2]
        outs[-1][...] = last_ref[...] + jnp.log(total_ref[...]) - pos_ref[...]
        outs = outs[2:]
    for n, k in enumerate(ks):
        p_ref, top_ref = ins[2 * n : 2 * n + 2]
        q_ref, mine_ref, other_ref = outs[3 * n : 3 * n + 3]
        own = mine_ref.shape[0]
        scale = jnp.exp(top_ref[...] - last_ref[...]) / total_ref[...]
        out = None
        for at in tiles(e_ref.shape[0]):
            q = (p_ref[:, at] * scale[:, at]).astype(BF16)
            if k == 0:
                hit = goal_ref[:, at] == lax.broadcasted_iota(jnp.int32, (own, q.shape[1]), 0)
                first = (q[:own].astype(F32) - jnp.where(hit, 1.0, 0.0)).astype(BF16)
                q = jnp.concatenate([first, q[own:]], axis=0)
            q_ref[:, at] = q
            part = jnp.dot(q, e_ref[at, :], preferred_element_type=F32)
            out = part if out is None else out + part
        mine_ref[...] = out[:own]
        other_ref[...] = out[own:].astype(BF16)


def share(ks, kept, last, total, e, *more):
    steps, rows = kept[ks[0]][0].shape
    width = e.shape[1]
    own = steps // 2
    each = [
        jax.ShapeDtypeStruct((steps, rows), BF16),
        jax.ShapeDtypeStruct((own, width), F32),
        jax.ShapeDtypeStruct((own, width), BF16),
    ]
    shapes = each * len(ks) + [jax.ShapeDtypeStruct((1, rows), F32)] * (0 in ks)
    ins = [part for k in ks for part in kept[k]]
    return pl.pallas_call(
        lambda *refs: share_kernel(ks, *refs),
        in_specs=[VMEM] * (3 + len(ins) + len(more)),
        out_specs=[VMEM] * len(shapes),
        out_shape=shapes,
        cost_estimate=cost(
            2 * len(ks) * steps * rows * width, len(ks) * 6 * steps * rows + 2 * rows * width
        ),
        compiler_params=params(24),
        name=f"share_{ks[0]}",
    )(last, total, e, *ins, *more)


def back_kernel(sizes, temper, *refs):
    n = len(sizes)
    w_ref, out_ref = refs[0], refs[-1]
    rows = None
    at = 1 + n
    for k in range(n):
        chunk = stack(refs[at : at + sizes[k]])
        at += sizes[k]
        part = lax.dot_general(refs[1 + k][...], chunk, TN, preferred_element_type=F32)
        rows = part if rows is None else rows + part
    out_ref[...] = lax.dot_general(
        (rows * temper).astype(BF16), w_ref[...], NT, preferred_element_type=F32
    ).astype(BF16)


def back(w, qs, chunks, temper):
    n = len(qs)
    steps, rows = qs[0].shape
    depth, width = w.shape
    tile = rows // 4
    flat = [part for chunk in chunks for part in chunk]
    return pl.pallas_call(
        lambda *refs: back_kernel([len(chunk) for chunk in chunks], temper, *refs),
        grid=(rows // tile,),
        in_specs=[pl.BlockSpec((depth, width), lambda i: (0, 0))]
        + [pl.BlockSpec((steps, tile), lambda i: (0, i))] * n
        + [pl.BlockSpec(part.shape, lambda i: (0, 0)) for part in flat],
        out_specs=pl.BlockSpec((tile, depth), lambda i: (i, 0)),
        out_shape=jax.ShapeDtypeStruct((rows, depth), BF16),
        cost_estimate=cost(
            2 * rows * width * (n * steps + depth),
            2 * (n * steps * (rows + width) + depth * width + rows * depth),
        ),
        compiler_params=params(40),
        name="back",
    )(w, *qs, *flat)


def shards(frames, w_frame, step_emb, targets, tile_frame, tile_step, tile_count):
    videos = lax.axis_size("vid")
    chips = videos // 2
    temper = 1.0 / math.sqrt(step_emb.shape[1])
    place = lax.axis_index("vid").astype(jnp.int32)

    def trade(x, k):
        return lax.ppermute(x, "vid", [(i, i ^ k) for i in range(videos)])

    goals = targets.reshape(1, -1)
    e = embed(frames, w_frame)
    found = trade(step_emb, 1)
    mine = {0: step_emb}
    for k in range(1, chips):
        mine[k] = trade(step_emb, 2 * k)
    mine[1], e = lax.optimization_barrier((mine[1], e))
    order = list(range(chips))
    chunks, kept = {}, {}
    more = (place.reshape(1), tile_count, tile_frame, tile_step, goals)
    for k in order:
        chunks[k] = [mine[k], found if k == 0 else trade(mine[k], 1)]
        if 0 < k < chips - 1:
            mine[k + 1], gate = lax.optimization_barrier((mine[k + 1], top))
        p, top, total, *first = score(k, videos, temper, e, chunks[k], *more)
        kept[k] = (p, top)
        if k == 0:
            pos, bias = first
        more = (bias, top, total)
    last = top

    qs, sums = {}, {}
    sequence = [(k,) for k in [*range(chips // 2, chips), *range(2, chips // 2)]] + [(1, 0)]
    for n, ks in enumerate(sequence):
        for m in range(n - 1, max(n - 3, -1), -1):
            k = sequence[m][0]
            if m == n - 1:
                e, qs[k] = lax.optimization_barrier((e, qs[k]))
            else:
                e, sums[k] = lax.optimization_barrier((e, sums[k]))
        made = share(ks, kept, last, total, e, *((goals, pos) if 0 in ks else ()))
        for m, k in enumerate(ks):
            qs[k], part, other = made[3 * m : 3 * m + 3]
            sums[k] = part + trade(other, 1).astype(F32)
    loss = made[-1]
    for ks in sequence:
        if ks[0] > 0:
            sums[ks[0]] = trade(sums[ks[0]].astype(BF16), 2 * ks[0])
    far = sequence[0][0]
    step_grad = sums[0]
    for k in range(1, chips):
        step_grad = step_grad + sums[k].astype(F32)
    frame_grad = back(
        w_frame, [qs[k] for k in order], [chunks[k] for k in order], temper
    )
    return (loss.reshape(-1), frame_grad, step_grad * temper)


def solution(mesh):
    placed = (
        P(("grp", "vid"), None),
        P(),
        P(("grp", "vid"), None),
        P(("grp", "vid")),
        P(("grp", "vid"), None),
        P(("grp", "vid"), None),
        P(("grp", "vid")),
    )
    return jax.shard_map(
        shards,
        mesh=mesh,
        in_specs=placed,
        out_specs=(P(("grp", "vid")), P(("grp", "vid"), None), P(("grp", "vid"), None)),
        check_vma=False,
    )
```

```python
import math

import jax
import jax.numpy as jnp
from jax import lax
from jax.experimental import pallas as pl
from jax.experimental.pallas import tpu as pltpu
from jax.sharding import PartitionSpec as P

F32 = jnp.float32
BF16 = jnp.bfloat16
HIDDEN = -1e30
EMBED_MIB = 52
TILES = 4
NT = (((1,), (1,)), ((), ()))
TN = (((0,), (0,)), ((), ()))
VMEM = pl.BlockSpec(memory_space=pltpu.VMEM)
SMEM = pl.BlockSpec(memory_space=pltpu.SMEM)


def params(mib):
    return pltpu.CompilerParams(vmem_limit_bytes=mib * 2**20)


def cost(flops, nbytes, exps=0, scale=1):
    return pl.CostEstimate(
        flops=flops // scale, bytes_accessed=nbytes // scale, transcendentals=exps // scale
    )


def embed_kernel(x_hbm, w_hbm, e_ref, x_ref, w_ref, sem):
    tile = x_ref.shape[0] // TILES
    deep = w_ref.shape[0] // TILES
    reads = []
    for n in range(TILES):
        at = pl.ds(n * deep, deep)
        reads.append(pltpu.make_async_copy(w_hbm.at[at], w_ref.at[at], sem.at[n]))
    for n in range(TILES):
        at = pl.ds(n * tile, tile)
        reads.append(pltpu.make_async_copy(x_hbm.at[at], x_ref.at[at], sem.at[TILES + n]))
    for read in reads:
        read.start()
    for read in reads[:TILES]:
        read.wait()
    for n in range(TILES):
        reads[TILES + n].wait()
        at = slice(n * tile, (n + 1) * tile)
        e_ref[at, :] = jnp.dot(x_ref[at, :], w_ref[...], preferred_element_type=F32).astype(BF16)


def embed(frames, w):
    rows, depth = frames.shape
    width = w.shape[1]
    return pl.pallas_call(
        embed_kernel,
        in_specs=[pl.BlockSpec(memory_space=pl.ANY)] * 2,
        out_specs=VMEM,
        out_shape=jax.ShapeDtypeStruct((rows, width), BF16),
        scratch_shapes=[
            pltpu.VMEM((rows, depth), BF16),
            pltpu.VMEM((depth, width), BF16),
            pltpu.SemaphoreType.DMA((2 * TILES,)),
        ],
        cost_estimate=cost(2 * rows * depth * width, 2 * (rows * depth + depth * width + rows * width)),
        compiler_params=params(EMBED_MIB),
        name="embed",
    )(frames, w)


def sight(place, count, tf, ts, shape):
    videos, rows = shape
    slots = tf.shape[1]
    line = lax.broadcasted_iota(jnp.int32, (videos, slots), 0)
    slot = lax.broadcasted_iota(jnp.int32, (videos, slots), 1)
    video = line ^ place
    left = jnp.where((ts == video) & (slot < count), 1.0, 0.0)
    block = lax.broadcasted_iota(jnp.int32, (rows, slots), 0) // 128
    right = jnp.where(tf == block, 1.0, 0.0)
    seen = lax.dot_general(left.astype(BF16), right.astype(BF16), NT, preferred_element_type=F32)
    return jnp.where(seen > 0.5, 0.0, HIDDEN)


def stack(refs):
    values = [ref[...] for ref in refs]
    return values[0] if len(values) == 1 else jnp.concatenate(values, axis=0)


def tiles(rows):
    return [slice(at, at + 256) for at in range(0, rows, 256)]


def score_kernel(k, parts, temper, *refs):
    e_ref = refs[0]
    blocks = refs[1 : 1 + parts]
    if k == 0:
        place_ref, count_ref, tf_ref, ts_ref, goal_ref = refs[1 + parts : 6 + parts]
        p_ref, top_ref, total_ref, pos_ref, bias_ref = refs[6 + parts :]
        bias_ref[...] = sight(place_ref[0], count_ref[0], tf_ref[...], ts_ref[...], bias_ref.shape)
    else:
        bias_ref, top_in, total_in, p_ref, top_ref, total_ref = refs[1 + parts :]
    chunk = stack(blocks)
    steps = chunk.shape[0]
    own = steps // 2
    for at in tiles(e_ref.shape[0]):
        s = lax.dot_general(chunk, e_ref[at, :], NT, preferred_element_type=F32) * temper
        bias = bias_ref[2 * k : 2 * k + 2, at]
        first, second = s[:own] + bias[0:1], s[own:] + bias[1:2]
        top = jnp.maximum(
            jnp.max(first, axis=0, keepdims=True), jnp.max(second, axis=0, keepdims=True)
        )
        if k == 0:
            hit = goal_ref[:, at] == lax.broadcasted_iota(jnp.int32, first.shape, 0)
            pos_ref[:, at] = jnp.sum(jnp.where(hit, s[:own], 0.0), axis=0, keepdims=True)
        else:
            top = jnp.maximum(top, top_in[:, at])
        first, second = jnp.exp(first - top), jnp.exp(second - top)
        p_ref[:own, at] = first
        p_ref[own:, at] = second
        total = jnp.sum(first, axis=0, keepdims=True) + jnp.sum(second, axis=0, keepdims=True)
        if k > 0:
            total = total + total_in[:, at] * jnp.exp(top_in[:, at] - top)
        top_ref[:, at] = top
        total_ref[:, at] = total


def score(k, videos, temper, e, chunk, *more):
    rows, width = e.shape
    steps = sum(part.shape[0] for part in chunk)
    line = jax.ShapeDtypeStruct((1, rows), F32)
    extra = [line, jax.ShapeDtypeStruct((videos, rows), F32)] if k == 0 else []
    specs = [SMEM, SMEM, VMEM, VMEM, VMEM] if k == 0 else [VMEM] * len(more)
    return pl.pallas_call(
        lambda *refs: score_kernel(k, len(chunk), temper, *refs),
        in_specs=[VMEM] * (1 + len(chunk)) + specs,
        out_specs=[VMEM] * (3 + len(extra)),
        out_shape=[jax.ShapeDtypeStruct((steps, rows), F32), line, line] + extra,
        cost_estimate=cost(
            2 * steps * rows * width, 2 * (rows + steps) * width + 4 * steps * rows, steps * rows
        ),
        compiler_params=params(24),
        name=f"score_{k}",
    )(e, *chunk, *more)


def share_kernel(ks, *refs):
    last_ref, total_ref, e_ref = refs[:3]
    ins, outs = refs[3 : 3 + 2 * len(ks)], refs[3 + 2 * len(ks) :]
    if 0 in ks:
        goal_ref, pos_ref = outs[:2]
        outs[-1][...] = last_ref[...] + jnp.log(total_ref[...]) - pos_ref[...]
        outs = outs[2:]
    for n, k in enumerate(ks):
        p_ref, top_ref = ins[2 * n : 2 * n + 2]
        q_ref, mine_ref, other_ref = outs[3 * n : 3 * n + 3]
        own = mine_ref.shape[0]
        scale = jnp.exp(top_ref[...] - last_ref[...]) / total_ref[...]
        out = None
        for at in tiles(e_ref.shape[0]):
            q = (p_ref[:, at] * scale[:, at]).astype(BF16)
            if k == 0:
                hit = goal_ref[:, at] == lax.broadcasted_iota(jnp.int32, (own, q.shape[1]), 0)
                first = (q[:own].astype(F32) - jnp.where(hit, 1.0, 0.0)).astype(BF16)
                q = jnp.concatenate([first, q[own:]], axis=0)
            q_ref[:, at] = q
            part = jnp.dot(q, e_ref[at, :], preferred_element_type=F32)
            out = part if out is None else out + part
        mine_ref[...] = out[:own]
        other_ref[...] = out[own:].astype(BF16)


def share(ks, kept, last, total, e, *more):
    steps, rows = kept[ks[0]][0].shape
    width = e.shape[1]
    own = steps // 2
    each = [
        jax.ShapeDtypeStruct((steps, rows), BF16),
        jax.ShapeDtypeStruct((own, width), F32),
        jax.ShapeDtypeStruct((own, width), BF16),
    ]
    shapes = each * len(ks) + [jax.ShapeDtypeStruct((1, rows), F32)] * (0 in ks)
    ins = [part for k in ks for part in kept[k]]
    return pl.pallas_call(
        lambda *refs: share_kernel(ks, *refs),
        in_specs=[VMEM] * (3 + len(ins) + len(more)),
        out_specs=[VMEM] * len(shapes),
        out_shape=shapes,
        cost_estimate=cost(
            2 * len(ks) * steps * rows * width, len(ks) * 6 * steps * rows + 2 * rows * width
        ),
        compiler_params=params(24),
        name=f"share_{ks[0]}",
    )(last, total, e, *ins, *more)


def rows_kernel(sizes, temper, *refs):
    n = len(sizes)
    out_ref = refs[-1]
    at = n
    chunks = []
    for size in sizes:
        chunks.append(stack(refs[at : at + size]))
        at += size
    for cut in tiles(out_ref.shape[0]):
        rows = None
        for q_ref, chunk in zip(refs[:n], chunks):
            part = lax.dot_general(q_ref[:, cut], chunk, TN, preferred_element_type=F32)
            rows = part if rows is None else rows + part
        out_ref[cut, :] = (rows * temper).astype(BF16)


def rows_of(qs, chunks, temper):
    n = len(qs)
    steps, rows = qs[0].shape
    flat = [part for chunk in chunks for part in chunk]
    width = flat[0].shape[1]
    return pl.pallas_call(
        lambda *refs: rows_kernel([len(chunk) for chunk in chunks], temper, *refs),
        in_specs=[VMEM] * (n + len(flat)),
        out_specs=VMEM,
        out_shape=jax.ShapeDtypeStruct((rows, width), BF16),
        cost_estimate=cost(2 * rows * width * n * steps, 2 * n * steps * (rows + width)),
        compiler_params=params(24),
        name="rows",
    )(*qs, *flat)


def back_kernel(g_ref, w_ref, out_ref):
    out_ref[...] = lax.dot_general(
        g_ref[...], w_ref[...], NT, preferred_element_type=F32
    ).astype(BF16)


def back(g, w):
    rows, width = g.shape
    depth = w.shape[0]
    tile = rows // 4
    return pl.pallas_call(
        back_kernel,
        grid=(rows // tile,),
        in_specs=[
            pl.BlockSpec((tile, width), lambda i: (i, 0)),
            pl.BlockSpec((depth, width), lambda i: (0, 0)),
        ],
        out_specs=pl.BlockSpec((tile, depth), lambda i: (i, 0)),
        out_shape=jax.ShapeDtypeStruct((rows, depth), BF16),
        cost_estimate=cost(2 * rows * width * depth, 2 * (depth * width + rows * (width + depth))),
        compiler_params=params(40),
        name="back",
    )(g, w)


def shards(frames, w_frame, step_emb, targets, tile_frame, tile_step, tile_count):
    videos = lax.axis_size("vid")
    chips = videos // 2
    temper = 1.0 / math.sqrt(step_emb.shape[1])
    place = lax.axis_index("vid").astype(jnp.int32)

    def trade(x, k):
        return lax.ppermute(x, "vid", [(i, i ^ k) for i in range(videos)])

    goals = targets.reshape(1, -1)
    e = embed(frames, w_frame)
    found = trade(step_emb, 1)
    mine = {0: step_emb}
    order = list(range(chips))
    chunks, kept = {}, {}
    more = (place.reshape(1), tile_count, tile_frame, tile_step, goals)
    for k in order:
        chunks[k] = [mine[k], found if k == 0 else trade(mine[k], 1)]
        if k + 1 < chips:
            low = (k + 1) & -(k + 1)
            come = trade(mine[k + 1 - low], 2 * low)
            mine[k + 1], gate = lax.optimization_barrier((come, e if k == 0 else top))
        p, top, total, *first = score(k, videos, temper, e, chunks[k], *more)
        kept[k] = (p, top)
        if k == 0:
            pos, bias = first
        more = (bias, top, total)
    last = top

    qs, sums = {}, {}
    sequence = [(k,) for k in range(chips - 1, 1, -1)] + [(1, 0)]
    for n, ks in enumerate(sequence):
        for m in range(n - 1, max(n - 3, -1), -1):
            k = sequence[m][0]
            if m == n - 1:
                e, qs[k] = lax.optimization_barrier((e, qs[k]))
            else:
                e, sums[k] = lax.optimization_barrier((e, sums[k]))
        made = share(ks, kept, last, total, e, *((goals, pos) if 0 in ks else ()))
        for m, k in enumerate(ks):
            qs[k], part, other = made[3 * m : 3 * m + 3]
            sums[k] = part + trade(other, 1).astype(F32)
    loss = made[-1]
    g = rows_of([qs[k] for k in order], [chunks[k] for k in order], temper)
    sums[1], g = lax.optimization_barrier((sums[1], g))
    bit = 1
    while bit < chips:
        for k in range(chips - bit, 0, -2 * bit):
            sums[k - bit] = sums[k - bit] + trade(sums[k].astype(BF16), 2 * bit).astype(F32)
        bit *= 2
    frame_grad = back(g, w_frame)
    return (loss.reshape(-1), frame_grad, sums[0] * temper)


def solution(mesh):
    placed = (
        P(("grp", "vid"), None),
        P(),
        P(("grp", "vid"), None),
        P(("grp", "vid")),
        P(("grp", "vid"), None),
        P(("grp", "vid"), None),
        P(("grp", "vid")),
    )
    return jax.shard_map(
        shards,
        mesh=mesh,
        in_specs=placed,
        out_specs=(P(("grp", "vid")), P(("grp", "vid"), None), P(("grp", "vid"), None)),
        check_vma=False,
    )
```

```python
import math

import jax
import jax.numpy as jnp
from jax import lax
from jax.experimental import pallas as pl
from jax.experimental.pallas import tpu as pltpu
from jax.sharding import PartitionSpec as P

F32 = jnp.float32
BF16 = jnp.bfloat16
HIDDEN = -1e30
EMBED_MIB = 51
TILES = 4
NT = (((1,), (1,)), ((), ()))
TN = (((0,), (0,)), ((), ()))
VMEM = pl.BlockSpec(memory_space=pltpu.VMEM)
SMEM = pl.BlockSpec(memory_space=pltpu.SMEM)


def params(mib):
    return pltpu.CompilerParams(vmem_limit_bytes=mib * 2**20)


def cost(flops, nbytes, exps=0, scale=1):
    return pl.CostEstimate(
        flops=flops // scale, bytes_accessed=nbytes // scale, transcendentals=exps // scale
    )


def embed_into(e_ref, x_hbm, w_hbm, x_ref, w_ref, small, sem):
    tile = x_ref.shape[0] // TILES
    deep = w_ref.shape[0] // TILES
    reads = []
    for n in range(TILES):
        at = pl.ds(n * deep, deep)
        reads.append(pltpu.make_async_copy(w_hbm.at[at], w_ref.at[at], sem.at[n]))
    for n in range(TILES):
        at = pl.ds(n * tile, tile)
        reads.append(pltpu.make_async_copy(x_hbm.at[at], x_ref.at[at], sem.at[TILES + n]))
    for n, (source, place) in enumerate(small):
        reads.append(pltpu.make_async_copy(source, place, sem.at[2 * TILES + n]))
    for read in reads:
        read.start()
    for read in reads[:TILES]:
        read.wait()
    for n in range(TILES):
        reads[TILES + n].wait()
        at = slice(n * tile, (n + 1) * tile)
        e_ref[at, :] = jnp.dot(x_ref[at, :], w_ref[...], preferred_element_type=F32).astype(BF16)
    for read in reads[2 * TILES :]:
        read.wait()


def sight(place, count, tf, ts, shape):
    videos, rows = shape
    slots = tf.shape[1]
    line = lax.broadcasted_iota(jnp.int32, (videos, slots), 0)
    slot = lax.broadcasted_iota(jnp.int32, (videos, slots), 1)
    video = line ^ place
    left = jnp.where((ts == video) & (slot < count), 1.0, 0.0)
    block = lax.broadcasted_iota(jnp.int32, (rows, slots), 0) // 128
    right = jnp.where(tf == block, 1.0, 0.0)
    seen = lax.dot_general(left.astype(BF16), right.astype(BF16), NT, preferred_element_type=F32)
    return jnp.where(seen > 0.5, 0.0, HIDDEN)


def stack(refs):
    values = [ref[...] for ref in refs]
    return values[0] if len(values) == 1 else jnp.concatenate(values, axis=0)


def tiles(rows):
    return [slice(at, at + 256) for at in range(0, rows, 256)]


def first_kernel(temper, *refs):
    x_hbm, w_hbm, *small, found_ref, place_ref = refs[:9]
    e_ref, p_ref, top_ref, total_ref, pos_ref, bias_ref = refs[9:15]
    x_ref, w_ref, *held, sem = refs[15:]
    own_ref, goal_ref, tf_ref, ts_ref, count_ref = held
    embed_into(e_ref, x_hbm, w_hbm, x_ref, w_ref, list(zip(small, held)), sem)
    bias_ref[...] = sight(place_ref[0], count_ref[...], tf_ref[...], ts_ref[...], bias_ref.shape)
    chunk = stack((own_ref, found_ref))
    scores(0, temper, chunk, e_ref, bias_ref, goal_ref, pos_ref, None, None, p_ref, top_ref, total_ref)


def first(temper, frames, w, small, found, place, videos):
    rows, depth = frames.shape
    width = w.shape[1]
    steps = 2 * found.shape[0]
    line = jax.ShapeDtypeStruct((1, rows), F32)
    anywhere = pl.BlockSpec(memory_space=pltpu.HBM)
    return pl.pallas_call(
        lambda *refs: first_kernel(temper, *refs),
        in_specs=[anywhere] * (2 + len(small)) + [VMEM, SMEM],
        out_specs=[VMEM] * 6,
        out_shape=[
            jax.ShapeDtypeStruct((rows, width), BF16),
            jax.ShapeDtypeStruct((steps, rows), F32),
            line,
            line,
            line,
            jax.ShapeDtypeStruct((videos, rows), F32),
        ],
        scratch_shapes=[pltpu.VMEM((rows, depth), BF16), pltpu.VMEM((depth, width), BF16)]
        + [pltpu.VMEM(part.shape, part.dtype) for part in small]
        + [pltpu.SemaphoreType.DMA((2 * TILES + len(small),))],
        cost_estimate=cost(
            2 * rows * width * (depth + steps), 2 * (rows * depth + depth * width + rows * width)
        ),
        compiler_params=params(EMBED_MIB),
        name="first",
    )(frames, w, *small, found, place)


def scores(k, temper, chunk, e_ref, bias_ref, goal_ref, pos_ref, top_in, total_in, p_ref, top_ref, total_ref):
    own = chunk.shape[0] // 2
    for at in tiles(e_ref.shape[0]):
        s = lax.dot_general(chunk, e_ref[at, :], NT, preferred_element_type=F32) * temper
        bias = bias_ref[2 * k : 2 * k + 2, at]
        first, second = s[:own] + bias[0:1], s[own:] + bias[1:2]
        top = jnp.maximum(
            jnp.max(first, axis=0, keepdims=True), jnp.max(second, axis=0, keepdims=True)
        )
        if k == 0:
            hit = goal_ref[:, at] == lax.broadcasted_iota(jnp.int32, first.shape, 0)
            pos_ref[:, at] = jnp.sum(jnp.where(hit, s[:own], 0.0), axis=0, keepdims=True)
        else:
            top = jnp.maximum(top, top_in[:, at])
        first, second = jnp.exp(first - top), jnp.exp(second - top)
        p_ref[:own, at] = first
        p_ref[own:, at] = second
        total = jnp.sum(first, axis=0, keepdims=True) + jnp.sum(second, axis=0, keepdims=True)
        if k > 0:
            total = total + total_in[:, at] * jnp.exp(top_in[:, at] - top)
        top_ref[:, at] = top
        total_ref[:, at] = total


def score_kernel(k, temper, *refs):
    e_ref, mine_ref, other_ref, bias_ref, top_in, total_in, p_ref, top_ref, total_ref = refs
    chunk = stack((mine_ref, other_ref))
    scores(k, temper, chunk, e_ref, bias_ref, None, None, top_in, total_in, p_ref, top_ref, total_ref)


def score(k, temper, e, chunk, bias, top, total):
    rows, width = e.shape
    steps = sum(part.shape[0] for part in chunk)
    line = jax.ShapeDtypeStruct((1, rows), F32)
    return pl.pallas_call(
        lambda *refs: score_kernel(k, temper, *refs),
        in_specs=[VMEM] * 6,
        out_specs=[VMEM] * 3,
        out_shape=[jax.ShapeDtypeStruct((steps, rows), F32), line, line],
        cost_estimate=cost(
            2 * steps * rows * width, 2 * (rows + steps) * width + 4 * steps * rows, steps * rows
        ),
        compiler_params=params(24),
        name=f"score_{k}",
    )(e, *chunk, bias, top, total)


def share_kernel(ks, *refs):
    last_ref, total_ref, e_ref = refs[:3]
    ins, outs = refs[3 : 3 + 2 * len(ks)], refs[3 + 2 * len(ks) :]
    if 0 in ks:
        goal_ref, pos_ref = outs[:2]
        outs[-1][...] = last_ref[...] + jnp.log(total_ref[...]) - pos_ref[...]
        outs = outs[2:]
    for n, k in enumerate(ks):
        p_ref, top_ref = ins[2 * n : 2 * n + 2]
        q_ref, mine_ref, other_ref = outs[3 * n : 3 * n + 3]
        own = mine_ref.shape[0]
        scale = jnp.exp(top_ref[...] - last_ref[...]) / total_ref[...]
        out = None
        for at in tiles(e_ref.shape[0]):
            q = (p_ref[:, at] * scale[:, at]).astype(BF16)
            if k == 0:
                hit = goal_ref[:, at] == lax.broadcasted_iota(jnp.int32, (own, q.shape[1]), 0)
                first = (q[:own].astype(F32) - jnp.where(hit, 1.0, 0.0)).astype(BF16)
                q = jnp.concatenate([first, q[own:]], axis=0)
            q_ref[:, at] = q
            part = jnp.dot(q, e_ref[at, :], preferred_element_type=F32)
            out = part if out is None else out + part
        mine_ref[...] = out[:own]
        other_ref[...] = out[own:].astype(BF16)


def share(ks, kept, last, total, e, *more):
    steps, rows = kept[ks[0]][0].shape
    width = e.shape[1]
    own = steps // 2
    each = [
        jax.ShapeDtypeStruct((steps, rows), BF16),
        jax.ShapeDtypeStruct((own, width), F32),
        jax.ShapeDtypeStruct((own, width), BF16),
    ]
    shapes = each * len(ks) + [jax.ShapeDtypeStruct((1, rows), F32)] * (0 in ks)
    ins = [part for k in ks for part in kept[k]]
    return pl.pallas_call(
        lambda *refs: share_kernel(ks, *refs),
        in_specs=[VMEM] * (3 + len(ins) + len(more)),
        out_specs=[VMEM] * len(shapes),
        out_shape=shapes,
        cost_estimate=cost(
            2 * len(ks) * steps * rows * width, len(ks) * 6 * steps * rows + 2 * rows * width
        ),
        compiler_params=params(24),
        name=f"share_{ks[0]}",
    )(last, total, e, *ins, *more)


def rows_kernel(sizes, temper, *refs):
    n = len(sizes)
    out_ref = refs[-1]
    at = n
    chunks = []
    for size in sizes:
        chunks.append(stack(refs[at : at + size]))
        at += size
    for cut in tiles(out_ref.shape[0]):
        rows = None
        for q_ref, chunk in zip(refs[:n], chunks):
            part = lax.dot_general(q_ref[:, cut], chunk, TN, preferred_element_type=F32)
            rows = part if rows is None else rows + part
        out_ref[cut, :] = (rows * temper).astype(BF16)


def rows_of(qs, chunks, temper):
    n = len(qs)
    steps, rows = qs[0].shape
    flat = [part for chunk in chunks for part in chunk]
    width = flat[0].shape[1]
    return pl.pallas_call(
        lambda *refs: rows_kernel([len(chunk) for chunk in chunks], temper, *refs),
        in_specs=[VMEM] * (n + len(flat)),
        out_specs=VMEM,
        out_shape=jax.ShapeDtypeStruct((rows, width), BF16),
        cost_estimate=cost(2 * rows * width * n * steps, 2 * n * steps * (rows + width)),
        compiler_params=params(24),
        name="rows",
    )(*qs, *flat)


def back_kernel(g_ref, w_ref, out_hbm, out_ref, sem):
    tile = out_ref.shape[0] // TILES
    writes = []
    for n in range(TILES):
        at = slice(n * tile, (n + 1) * tile)
        out_ref[at, :] = lax.dot_general(
            g_ref[at, :], w_ref[...], NT, preferred_element_type=F32
        ).astype(BF16)
        at = pl.ds(n * tile, tile)
        writes.append(pltpu.make_async_copy(out_ref.at[at], out_hbm.at[at], sem.at[n]))
        writes[n].start()
    for write in writes:
        write.wait()


def back(g, w):
    rows, width = g.shape
    depth = w.shape[0]
    return pl.pallas_call(
        back_kernel,
        in_specs=[VMEM, VMEM],
        out_specs=pl.BlockSpec(memory_space=pl.ANY),
        out_shape=jax.ShapeDtypeStruct((rows, depth), BF16),
        scratch_shapes=[pltpu.VMEM((rows, depth), BF16), pltpu.SemaphoreType.DMA((TILES,))],
        cost_estimate=cost(2 * rows * width * depth, 2 * (depth * width + rows * (width + depth))),
        compiler_params=params(40),
        name="back",
    )(g, w)


def shards(frames, w_frame, step_emb, targets, tile_frame, tile_step, tile_count):
    videos = lax.axis_size("vid")
    chips = videos // 2
    temper = 1.0 / math.sqrt(step_emb.shape[1])
    place = lax.axis_index("vid").astype(jnp.int32)

    def trade(x, k):
        return lax.ppermute(x, "vid", [(i, i ^ k) for i in range(videos)])

    goals = targets.reshape(1, -1)
    found = trade(step_emb, 1)
    order = list(range(chips))
    chunks, kept = {0: [step_emb, found]}, {}
    come = {k: trade(step_emb, 2 * k) for k in range(2, chips)}
    come[1] = trade(found, 2)
    small = (step_emb, goals, tile_frame, tile_step, tile_count.reshape(1, 1))
    e, p, top, total, pos, bias = first(
        temper, frames, w_frame, small, found, place.reshape(1), videos
    )
    kept[0] = (p, top)
    for k in range(1, chips):
        if k <= 2:
            come[k], gate = lax.optimization_barrier((come[k], e))
        if k == 1:
            chunks[1] = [trade(come[1], 1), come[1]]
            continue
        chunks[k] = [come[k], trade(come[k], 1)]
        if k + 1 < chips:
            come[k + 1], gate = lax.optimization_barrier((come[k + 1], top))
        p, top, total = score(k - 1, temper, e, chunks[k - 1], bias, top, total)
        kept[k - 1] = (p, top)
        if k + 1 < chips:
            come[k + 1], gate = lax.optimization_barrier((come[k + 1], top))
    p, top, total = score(chips - 1, temper, e, chunks[chips - 1], bias, top, total)
    kept[chips - 1] = (p, top)
    last = top

    qs, sums = {}, {}
    sequence = [(k,) for k in range(chips - 1, 1, -1)] + [(1, 0)]
    for n, ks in enumerate(sequence):
        for m in range(n - 1, max(n - 3, -1), -1):
            k = sequence[m][0]
            if m == n - 1:
                e, qs[k] = lax.optimization_barrier((e, qs[k]))
            else:
                e, sums[k] = lax.optimization_barrier((e, sums[k]))
        made = share(ks, kept, last, total, e, *((goals, pos) if 0 in ks else ()))
        for m, k in enumerate(ks):
            qs[k], part, other = made[3 * m : 3 * m + 3]
            sums[k] = part + trade(other, 1).astype(F32)
    loss = made[-1]
    g = rows_of([qs[k] for k in order], [chunks[k] for k in order], temper)
    sums[1], g = lax.optimization_barrier((sums[1], g))
    bit = 1
    while bit < chips:
        for k in range(chips - bit, 0, -2 * bit):
            sums[k - bit] = sums[k - bit] + trade(sums[k].astype(BF16), 2 * bit).astype(F32)
        bit *= 2
    frame_grad = back(g, w_frame)
    return (loss.reshape(-1), frame_grad, sums[0] * temper)


def solution(mesh):
    placed = (
        P(("grp", "vid"), None),
        P(),
        P(("grp", "vid"), None),
        P(("grp", "vid")),
        P(("grp", "vid"), None),
        P(("grp", "vid"), None),
        P(("grp", "vid")),
    )
    return jax.shard_map(
        shards,
        mesh=mesh,
        in_specs=placed,
        out_specs=(P(("grp", "vid")), P(("grp", "vid"), None), P(("grp", "vid"), None)),
        check_vma=False,
    )
```

```python
import math

import jax
import jax.numpy as jnp
from jax import lax
from jax.experimental import pallas as pl
from jax.experimental.pallas import tpu as pltpu
from jax.sharding import PartitionSpec as P

F32 = jnp.float32
BF16 = jnp.bfloat16
HIDDEN = -1e30
EMBED_MIB = 52
TILES = 4
NT = (((1,), (1,)), ((), ()))
TN = (((0,), (0,)), ((), ()))
VMEM = pl.BlockSpec(memory_space=pltpu.VMEM)
SMEM = pl.BlockSpec(memory_space=pltpu.SMEM)


def params(mib):
    return pltpu.CompilerParams(vmem_limit_bytes=mib * 2**20)


def cost(flops, nbytes, exps=0, scale=1):
    return pl.CostEstimate(
        flops=flops // scale, bytes_accessed=nbytes // scale, transcendentals=exps // scale
    )


def embed_kernel(x_hbm, w_hbm, e_ref, x_ref, w_ref, sem):
    tile = x_ref.shape[0] // TILES
    deep = w_ref.shape[0] // TILES
    reads = []
    for n in range(TILES):
        at = pl.ds(n * deep, deep)
        reads.append(pltpu.make_async_copy(w_hbm.at[at], w_ref.at[at], sem.at[n]))
    for n in range(TILES):
        at = pl.ds(n * tile, tile)
        reads.append(pltpu.make_async_copy(x_hbm.at[at], x_ref.at[at], sem.at[TILES + n]))
    for read in reads:
        read.start()
    for read in reads[:TILES]:
        read.wait()
    for n in range(TILES):
        reads[TILES + n].wait()
        at = slice(n * tile, (n + 1) * tile)
        e_ref[at, :] = jnp.dot(x_ref[at, :], w_ref[...], preferred_element_type=F32).astype(BF16)


def embed(frames, w):
    rows, depth = frames.shape
    width = w.shape[1]
    return pl.pallas_call(
        embed_kernel,
        in_specs=[pl.BlockSpec(memory_space=pl.ANY)] * 2,
        out_specs=VMEM,
        out_shape=jax.ShapeDtypeStruct((rows, width), BF16),
        scratch_shapes=[
            pltpu.VMEM((rows, depth), BF16),
            pltpu.VMEM((depth, width), BF16),
            pltpu.SemaphoreType.DMA((2 * TILES,)),
        ],
        cost_estimate=cost(2 * rows * depth * width, 2 * (rows * depth + depth * width + rows * width)),
        compiler_params=params(EMBED_MIB),
        name="embed",
    )(frames, w)


def sight(place, count, tf, ts, shape):
    videos, rows = shape
    slots = tf.shape[1]
    line = lax.broadcasted_iota(jnp.int32, (videos, slots), 0)
    slot = lax.broadcasted_iota(jnp.int32, (videos, slots), 1)
    video = line ^ place
    left = jnp.where((ts == video) & (slot < count), 1.0, 0.0)
    block = lax.broadcasted_iota(jnp.int32, (rows, slots), 0) // 128
    right = jnp.where(tf == block, 1.0, 0.0)
    seen = lax.dot_general(left.astype(BF16), right.astype(BF16), NT, preferred_element_type=F32)
    return jnp.where(seen > 0.5, 0.0, HIDDEN)


def stack(refs):
    values = [ref[...] for ref in refs]
    return values[0] if len(values) == 1 else jnp.concatenate(values, axis=0)


def tiles(rows):
    return [slice(at, at + 256) for at in range(0, rows, 256)]


def score_kernel(k, parts, temper, *refs):
    e_ref = refs[0]
    blocks = refs[1 : 1 + parts]
    if k == 0:
        place_ref, count_ref, tf_ref, ts_ref, goal_ref = refs[1 + parts : 6 + parts]
        p_ref, top_ref, total_ref, pos_ref, bias_ref = refs[6 + parts :]
        bias_ref[...] = sight(place_ref[0], count_ref[0], tf_ref[...], ts_ref[...], bias_ref.shape)
    else:
        bias_ref, top_in, total_in, p_ref, top_ref, total_ref = refs[1 + parts :]
    chunk = stack(blocks)
    steps = chunk.shape[0]
    own = steps // 2
    for at in tiles(e_ref.shape[0]):
        s = lax.dot_general(chunk, e_ref[at, :], NT, preferred_element_type=F32) * temper
        bias = bias_ref[2 * k : 2 * k + 2, at]
        first, second = s[:own] + bias[0:1], s[own:] + bias[1:2]
        top = jnp.maximum(
            jnp.max(first, axis=0, keepdims=True), jnp.max(second, axis=0, keepdims=True)
        )
        if k == 0:
            hit = goal_ref[:, at] == lax.broadcasted_iota(jnp.int32, first.shape, 0)
            pos_ref[:, at] = jnp.sum(jnp.where(hit, s[:own], 0.0), axis=0, keepdims=True)
        else:
            top = jnp.maximum(top, top_in[:, at])
        first, second = jnp.exp(first - top), jnp.exp(second - top)
        p_ref[:own, at] = first
        p_ref[own:, at] = second
        total = jnp.sum(first, axis=0, keepdims=True) + jnp.sum(second, axis=0, keepdims=True)
        if k > 0:
            total = total + total_in[:, at] * jnp.exp(top_in[:, at] - top)
        top_ref[:, at] = top
        total_ref[:, at] = total


def score(k, videos, temper, e, chunk, *more):
    rows, width = e.shape
    steps = sum(part.shape[0] for part in chunk)
    line = jax.ShapeDtypeStruct((1, rows), F32)
    extra = [line, jax.ShapeDtypeStruct((videos, rows), F32)] if k == 0 else []
    specs = [SMEM, SMEM, VMEM, VMEM, VMEM] if k == 0 else [VMEM] * len(more)
    return pl.pallas_call(
        lambda *refs: score_kernel(k, len(chunk), temper, *refs),
        in_specs=[VMEM] * (1 + len(chunk)) + specs,
        out_specs=[VMEM] * (3 + len(extra)),
        out_shape=[jax.ShapeDtypeStruct((steps, rows), F32), line, line] + extra,
        cost_estimate=cost(
            2 * steps * rows * width, 2 * (rows + steps) * width + 4 * steps * rows, steps * rows
        ),
        compiler_params=params(24),
        name=f"score_{k}",
    )(e, *chunk, *more)


def share_kernel(ks, *refs):
    last_ref, total_ref, e_ref = refs[:3]
    ins, outs = refs[3 : 3 + 2 * len(ks)], refs[3 + 2 * len(ks) :]
    if 0 in ks:
        goal_ref, pos_ref = outs[:2]
        outs[-1][...] = last_ref[...] + jnp.log(total_ref[...]) - pos_ref[...]
        outs = outs[2:]
    for n, k in enumerate(ks):
        p_ref, top_ref = ins[2 * n : 2 * n + 2]
        q_ref, mine_ref, other_ref = outs[3 * n : 3 * n + 3]
        own = mine_ref.shape[0]
        scale = jnp.exp(top_ref[...] - last_ref[...]) / total_ref[...]
        out = None
        for at in tiles(e_ref.shape[0]):
            q = (p_ref[:, at] * scale[:, at]).astype(BF16)
            if k == 0:
                hit = goal_ref[:, at] == lax.broadcasted_iota(jnp.int32, (own, q.shape[1]), 0)
                first = (q[:own].astype(F32) - jnp.where(hit, 1.0, 0.0)).astype(BF16)
                q = jnp.concatenate([first, q[own:]], axis=0)
            q_ref[:, at] = q
            part = jnp.dot(q, e_ref[at, :], preferred_element_type=F32)
            out = part if out is None else out + part
        mine_ref[...] = out[:own]
        other_ref[...] = out[own:].astype(BF16)


def share(ks, kept, last, total, e, *more):
    steps, rows = kept[ks[0]][0].shape
    width = e.shape[1]
    own = steps // 2
    each = [
        jax.ShapeDtypeStruct((steps, rows), BF16),
        jax.ShapeDtypeStruct((own, width), F32),
        jax.ShapeDtypeStruct((own, width), BF16),
    ]
    shapes = each * len(ks) + [jax.ShapeDtypeStruct((1, rows), F32)] * (0 in ks)
    ins = [part for k in ks for part in kept[k]]
    return pl.pallas_call(
        lambda *refs: share_kernel(ks, *refs),
        in_specs=[VMEM] * (3 + len(ins) + len(more)),
        out_specs=[VMEM] * len(shapes),
        out_shape=shapes,
        cost_estimate=cost(
            2 * len(ks) * steps * rows * width, len(ks) * 6 * steps * rows + 2 * rows * width
        ),
        compiler_params=params(24),
        name=f"share_{ks[0]}",
    )(last, total, e, *ins, *more)


def rows_kernel(sizes, temper, *refs):
    n = len(sizes)
    out_ref = refs[-1]
    at = n
    chunks = []
    for size in sizes:
        chunks.append(stack(refs[at : at + size]))
        at += size
    for cut in tiles(out_ref.shape[0]):
        rows = None
        for q_ref, chunk in zip(refs[:n], chunks):
            part = lax.dot_general(q_ref[:, cut], chunk, TN, preferred_element_type=F32)
            rows = part if rows is None else rows + part
        out_ref[cut, :] = (rows * temper).astype(BF16)


def rows_of(qs, chunks, temper):
    n = len(qs)
    steps, rows = qs[0].shape
    flat = [part for chunk in chunks for part in chunk]
    width = flat[0].shape[1]
    return pl.pallas_call(
        lambda *refs: rows_kernel([len(chunk) for chunk in chunks], temper, *refs),
        in_specs=[VMEM] * (n + len(flat)),
        out_specs=VMEM,
        out_shape=jax.ShapeDtypeStruct((rows, width), BF16),
        cost_estimate=cost(2 * rows * width * n * steps, 2 * n * steps * (rows + width)),
        compiler_params=params(24),
        name="rows",
    )(*qs, *flat)


def back_kernel(g_ref, w_ref, out_hbm, out_ref, sem):
    tile = out_ref.shape[0] // TILES
    writes = []
    for n in range(TILES):
        at = slice(n * tile, (n + 1) * tile)
        out_ref[at, :] = lax.dot_general(
            g_ref[at, :], w_ref[...], NT, preferred_element_type=F32
        ).astype(BF16)
        at = pl.ds(n * tile, tile)
        writes.append(pltpu.make_async_copy(out_ref.at[at], out_hbm.at[at], sem.at[n]))
        writes[n].start()
    for write in writes:
        write.wait()


def back(g, w):
    rows, width = g.shape
    depth = w.shape[0]
    return pl.pallas_call(
        back_kernel,
        in_specs=[VMEM, VMEM],
        out_specs=pl.BlockSpec(memory_space=pl.ANY),
        out_shape=jax.ShapeDtypeStruct((rows, depth), BF16),
        scratch_shapes=[pltpu.VMEM((rows, depth), BF16), pltpu.SemaphoreType.DMA((TILES,))],
        cost_estimate=cost(2 * rows * width * depth, 2 * (depth * width + rows * (width + depth))),
        compiler_params=params(40),
        name="back",
    )(g, w)


def shards(frames, w_frame, step_emb, targets, tile_frame, tile_step, tile_count):
    videos = lax.axis_size("vid")
    chips = videos // 2
    temper = 1.0 / math.sqrt(step_emb.shape[1])
    place = lax.axis_index("vid").astype(jnp.int32)

    def trade(x, k):
        return lax.ppermute(x, "vid", [(i, i ^ k) for i in range(videos)])

    goals = targets.reshape(1, -1)
    e = embed(frames, w_frame)
    found = trade(step_emb, 1)
    mine = {0: step_emb}
    order, bit = [0], chips // 2
    while bit:
        order += [k ^ bit for k in order]
        bit //= 2
    chunks, kept = {}, {}
    more = (place.reshape(1), tile_count, tile_frame, tile_step, goals)
    for n, k in enumerate(order):
        chunks[k] = [mine[k], found if k == 0 else trade(mine[k], 1)]
        if n + 1 < chips:
            coming = order[n + 1]
            low = coming & -coming
            come = trade(mine[coming ^ low], 2 * low)
            mine[coming], gate = lax.optimization_barrier((come, e if n == 0 else top))
        p, top, total, *first = score(k, videos, temper, e, chunks[k], *more)
        kept[k] = (p, top)
        if k == 0:
            pos, bias = first
        more = (bias, top, total)
    last = top

    qs, sums = {}, {}
    sequence = [(k,) for k in range(chips - 1, 1, -1)] + [(1, 0)]
    for n, ks in enumerate(sequence):
        for m in range(n - 1, max(n - 3, -1), -1):
            k = sequence[m][0]
            if m == n - 1:
                e, qs[k] = lax.optimization_barrier((e, qs[k]))
            else:
                e, sums[k] = lax.optimization_barrier((e, sums[k]))
        made = share(ks, kept, last, total, e, *((goals, pos) if 0 in ks else ()))
        for m, k in enumerate(ks):
            qs[k], part, other = made[3 * m : 3 * m + 3]
            sums[k] = part + trade(other, 1).astype(F32)
    loss = made[-1]
    g = rows_of([qs[k] for k in order], [chunks[k] for k in order], temper)
    sums[1], g = lax.optimization_barrier((sums[1], g))
    bit = 1
    while bit < chips:
        for k in range(chips - bit, 0, -2 * bit):
            sums[k - bit] = sums[k - bit] + trade(sums[k].astype(BF16), 2 * bit).astype(F32)
        bit *= 2
    frame_grad = back(g, w_frame)
    return (loss.reshape(-1), frame_grad, sums[0] * temper)


def solution(mesh):
    placed = (
        P(("grp", "vid"), None),
        P(),
        P(("grp", "vid"), None),
        P(("grp", "vid")),
        P(("grp", "vid"), None),
        P(("grp", "vid"), None),
        P(("grp", "vid")),
    )
    return jax.shard_map(
        shards,
        mesh=mesh,
        in_specs=placed,
        out_specs=(P(("grp", "vid")), P(("grp", "vid"), None), P(("grp", "vid"), None)),
        check_vma=False,
    )
```

```python
import math

import jax
import jax.numpy as jnp
from jax import lax
from jax.experimental import pallas as pl
from jax.experimental.pallas import tpu as pltpu
from jax.sharding import PartitionSpec as P

F32 = jnp.float32
BF16 = jnp.bfloat16
HIDDEN = -1e30
EMBED_MIB = 52
TILES = 4
NT = (((1,), (1,)), ((), ()))
TN = (((0,), (0,)), ((), ()))
VMEM = pl.BlockSpec(memory_space=pltpu.VMEM)
SMEM = pl.BlockSpec(memory_space=pltpu.SMEM)


def params(mib):
    return pltpu.CompilerParams(vmem_limit_bytes=mib * 2**20)


def cost(flops, nbytes, exps=0, scale=1):
    return pl.CostEstimate(
        flops=flops // scale, bytes_accessed=nbytes // scale, transcendentals=exps // scale
    )


def embed_kernel(x_hbm, w_hbm, e_ref, x_ref, w_ref, sem):
    tile = x_ref.shape[0] // TILES
    deep = w_ref.shape[0] // TILES
    reads = []
    for n in range(TILES):
        at = pl.ds(n * deep, deep)
        reads.append(pltpu.make_async_copy(w_hbm.at[at], w_ref.at[at], sem.at[n]))
    for n in range(TILES):
        at = pl.ds(n * tile, tile)
        reads.append(pltpu.make_async_copy(x_hbm.at[at], x_ref.at[at], sem.at[TILES + n]))
    for read in reads:
        read.start()
    for read in reads[:TILES]:
        read.wait()
    for n in range(TILES):
        reads[TILES + n].wait()
        at = slice(n * tile, (n + 1) * tile)
        e_ref[at, :] = jnp.dot(x_ref[at, :], w_ref[...], preferred_element_type=F32).astype(BF16)


def embed(frames, w):
    rows, depth = frames.shape
    width = w.shape[1]
    return pl.pallas_call(
        embed_kernel,
        in_specs=[pl.BlockSpec(memory_space=pl.ANY)] * 2,
        out_specs=VMEM,
        out_shape=jax.ShapeDtypeStruct((rows, width), BF16),
        scratch_shapes=[
            pltpu.VMEM((rows, depth), BF16),
            pltpu.VMEM((depth, width), BF16),
            pltpu.SemaphoreType.DMA((2 * TILES,)),
        ],
        cost_estimate=cost(2 * rows * depth * width, 2 * (rows * depth + depth * width + rows * width)),
        compiler_params=params(EMBED_MIB),
        name="embed",
    )(frames, w)


def sight(place, count, tf, ts, shape):
    videos, rows = shape
    slots = tf.shape[1]
    line = lax.broadcasted_iota(jnp.int32, (videos, slots), 0)
    slot = lax.broadcasted_iota(jnp.int32, (videos, slots), 1)
    video = line ^ place
    left = jnp.where((ts == video) & (slot < count), 1.0, 0.0)
    block = lax.broadcasted_iota(jnp.int32, (rows, slots), 0) // 128
    right = jnp.where(tf == block, 1.0, 0.0)
    seen = lax.dot_general(left.astype(BF16), right.astype(BF16), NT, preferred_element_type=F32)
    return jnp.where(seen > 0.5, 0.0, HIDDEN)


def stack(refs):
    values = [ref[...] for ref in refs]
    return values[0] if len(values) == 1 else jnp.concatenate(values, axis=0)


def tiles(rows):
    return [slice(at, at + 256) for at in range(0, rows, 256)]


def score_kernel(k, parts, temper, *refs):
    e_ref = refs[0]
    blocks = refs[1 : 1 + parts]
    if k == 0:
        place_ref, count_ref, tf_ref, ts_ref, goal_ref = refs[1 + parts : 6 + parts]
        p_ref, top_ref, total_ref, pos_ref, bias_ref = refs[6 + parts :]
        bias_ref[...] = sight(place_ref[0], count_ref[0], tf_ref[...], ts_ref[...], bias_ref.shape)
    else:
        bias_ref, top_in, total_in, p_ref, top_ref, total_ref = refs[1 + parts :]
    chunk = stack(blocks)
    steps = chunk.shape[0]
    own = steps // 2
    for at in tiles(e_ref.shape[0]):
        s = lax.dot_general(chunk, e_ref[at, :], NT, preferred_element_type=F32) * temper
        bias = bias_ref[2 * k : 2 * k + 2, at]
        first, second = s[:own] + bias[0:1], s[own:] + bias[1:2]
        top = jnp.maximum(
            jnp.max(first, axis=0, keepdims=True), jnp.max(second, axis=0, keepdims=True)
        )
        if k == 0:
            hit = goal_ref[:, at] == lax.broadcasted_iota(jnp.int32, first.shape, 0)
            pos_ref[:, at] = jnp.sum(jnp.where(hit, s[:own], 0.0), axis=0, keepdims=True)
        else:
            top = jnp.maximum(top, top_in[:, at])
        first, second = jnp.exp(first - top), jnp.exp(second - top)
        p_ref[:own, at] = first
        p_ref[own:, at] = second
        total = jnp.sum(first, axis=0, keepdims=True) + jnp.sum(second, axis=0, keepdims=True)
        if k > 0:
            total = total + total_in[:, at] * jnp.exp(top_in[:, at] - top)
        top_ref[:, at] = top
        total_ref[:, at] = total


def score(k, videos, temper, e, chunk, *more):
    rows, width = e.shape
    steps = sum(part.shape[0] for part in chunk)
    line = jax.ShapeDtypeStruct((1, rows), F32)
    extra = [line, jax.ShapeDtypeStruct((videos, rows), F32)] if k == 0 else []
    specs = [SMEM, SMEM, VMEM, VMEM, VMEM] if k == 0 else [VMEM] * len(more)
    return pl.pallas_call(
        lambda *refs: score_kernel(k, len(chunk), temper, *refs),
        in_specs=[VMEM] * (1 + len(chunk)) + specs,
        out_specs=[VMEM] * (3 + len(extra)),
        out_shape=[jax.ShapeDtypeStruct((steps, rows), F32), line, line] + extra,
        cost_estimate=cost(
            2 * steps * rows * width, 2 * (rows + steps) * width + 4 * steps * rows, steps * rows
        ),
        compiler_params=params(24),
        name=f"score_{k}",
    )(e, *chunk, *more)


def share_kernel(ks, *refs):
    last_ref, total_ref, e_ref = refs[:3]
    ins, outs = refs[3 : 3 + 2 * len(ks)], refs[3 + 2 * len(ks) :]
    if 0 in ks:
        goal_ref, pos_ref = outs[:2]
        outs[-1][...] = last_ref[...] + jnp.log(total_ref[...]) - pos_ref[...]
        outs = outs[2:]
    for n, k in enumerate(ks):
        p_ref, top_ref = ins[2 * n : 2 * n + 2]
        q_ref, mine_ref, other_ref = outs[3 * n : 3 * n + 3]
        own = mine_ref.shape[0]
        scale = jnp.exp(top_ref[...] - last_ref[...]) / total_ref[...]
        out = None
        for at in tiles(e_ref.shape[0]):
            q = (p_ref[:, at] * scale[:, at]).astype(BF16)
            if k == 0:
                hit = goal_ref[:, at] == lax.broadcasted_iota(jnp.int32, (own, q.shape[1]), 0)
                first = (q[:own].astype(F32) - jnp.where(hit, 1.0, 0.0)).astype(BF16)
                q = jnp.concatenate([first, q[own:]], axis=0)
            q_ref[:, at] = q
            part = jnp.dot(q, e_ref[at, :], preferred_element_type=F32)
            out = part if out is None else out + part
        mine_ref[...] = out[:own]
        other_ref[...] = out[own:].astype(BF16)


def share(ks, kept, last, total, e, *more):
    steps, rows = kept[ks[0]][0].shape
    width = e.shape[1]
    own = steps // 2
    each = [
        jax.ShapeDtypeStruct((steps, rows), BF16),
        jax.ShapeDtypeStruct((own, width), F32),
        jax.ShapeDtypeStruct((own, width), BF16),
    ]
    shapes = each * len(ks) + [jax.ShapeDtypeStruct((1, rows), F32)] * (0 in ks)
    ins = [part for k in ks for part in kept[k]]
    return pl.pallas_call(
        lambda *refs: share_kernel(ks, *refs),
        in_specs=[VMEM] * (3 + len(ins) + len(more)),
        out_specs=[VMEM] * len(shapes),
        out_shape=shapes,
        cost_estimate=cost(
            2 * len(ks) * steps * rows * width, len(ks) * 6 * steps * rows + 2 * rows * width
        ),
        compiler_params=params(24),
        name=f"share_{ks[0]}",
    )(last, total, e, *ins, *more)


def rows_kernel(sizes, temper, *refs):
    n = len(sizes)
    out_ref = refs[-1]
    at = n
    chunks = []
    for size in sizes:
        chunks.append(stack(refs[at : at + size]))
        at += size
    for cut in tiles(out_ref.shape[0]):
        rows = None
        for q_ref, chunk in zip(refs[:n], chunks):
            part = lax.dot_general(q_ref[:, cut], chunk, TN, preferred_element_type=F32)
            rows = part if rows is None else rows + part
        out_ref[cut, :] = (rows * temper).astype(BF16)


def rows_of(qs, chunks, temper):
    n = len(qs)
    steps, rows = qs[0].shape
    flat = [part for chunk in chunks for part in chunk]
    width = flat[0].shape[1]
    return pl.pallas_call(
        lambda *refs: rows_kernel([len(chunk) for chunk in chunks], temper, *refs),
        in_specs=[VMEM] * (n + len(flat)),
        out_specs=VMEM,
        out_shape=jax.ShapeDtypeStruct((rows, width), BF16),
        cost_estimate=cost(2 * rows * width * n * steps, 2 * n * steps * (rows + width)),
        compiler_params=params(24),
        name="rows",
    )(*qs, *flat)


def back_kernel(g_ref, w_ref, out_hbm, out_ref, sem):
    tile = out_ref.shape[0] // TILES
    writes = []
    for n in range(TILES):
        at = slice(n * tile, (n + 1) * tile)
        out_ref[at, :] = lax.dot_general(
            g_ref[at, :], w_ref[...], NT, preferred_element_type=F32
        ).astype(BF16)
        at = pl.ds(n * tile, tile)
        writes.append(pltpu.make_async_copy(out_ref.at[at], out_hbm.at[at], sem.at[n]))
        writes[n].start()
    for write in writes:
        write.wait()


def back(g, w):
    rows, width = g.shape
    depth = w.shape[0]
    return pl.pallas_call(
        back_kernel,
        in_specs=[VMEM, VMEM],
        out_specs=pl.BlockSpec(memory_space=pl.ANY),
        out_shape=jax.ShapeDtypeStruct((rows, depth), BF16),
        scratch_shapes=[pltpu.VMEM((rows, depth), BF16), pltpu.SemaphoreType.DMA((TILES,))],
        cost_estimate=cost(2 * rows * width * depth, 2 * (depth * width + rows * (width + depth))),
        compiler_params=params(40),
        name="back",
    )(g, w)


def shards(frames, w_frame, step_emb, targets, tile_frame, tile_step, tile_count):
    videos = lax.axis_size("vid")
    chips = videos // 2
    temper = 1.0 / math.sqrt(step_emb.shape[1])
    place = lax.axis_index("vid").astype(jnp.int32)

    def trade(x, k):
        return lax.ppermute(x, "vid", [(i, i ^ k) for i in range(videos)])

    goals = targets.reshape(1, -1)
    e = embed(frames, w_frame)
    found = trade(step_emb, 1)
    mine = {0: step_emb}
    order, bit = [0], chips // 2
    while bit:
        order += [k ^ bit for k in order]
        bit //= 2
    chunks, kept = {}, {}
    more = (place.reshape(1), tile_count, tile_frame, tile_step, goals)
    for n, k in enumerate(order):
        chunks[k] = [mine[k], found if k == 0 else trade(mine[k], 1)]
        if n + 1 < chips:
            coming = order[n + 1]
            low = coming & -coming
            come = trade(mine[coming ^ low], 2 * low)
            mine[coming], gate = lax.optimization_barrier((come, e if n == 0 else top))
        p, top, total, *first = score(k, videos, temper, e, chunks[k], *more)
        kept[k] = (p, top)
        if k == 0:
            pos, bias = first
        more = (bias, top, total)
    last = top

    qs, sums = {}, {}
    sequence = [(k,) for k in range(chips - 1, 1, -1)] + [(1, 0)]
    for n, ks in enumerate(sequence):
        for m in range(n - 1, max(n - 3, -1), -1):
            k = sequence[m][0]
            if m == n - 1:
                e, qs[k] = lax.optimization_barrier((e, qs[k]))
            else:
                e, sums[k] = lax.optimization_barrier((e, sums[k]))
        made = share(ks, kept, last, total, e, *((goals, pos) if 0 in ks else ()))
        for m, k in enumerate(ks):
            qs[k], part, other = made[3 * m : 3 * m + 3]
            sums[k] = part + trade(other, 1).astype(F32)
    loss = made[-1]
    g = rows_of([qs[k] for k in order], [chunks[k] for k in order], temper)
    sums[1], g = lax.optimization_barrier((sums[1], g))
    bit = 1
    while bit < chips:
        for k in range(chips - bit, 0, -2 * bit):
            if bit == 1 and k > 1:
                cut = sums[k].shape[0] // 2
                moved = [
                    sums[k - 1][at] + trade(sums[k][at].astype(BF16), 2).astype(F32)
                    for at in (slice(None, cut), slice(cut, None))
                ]
                sums[k - 1] = jnp.concatenate(moved, axis=0)
                continue
            sums[k - bit] = sums[k - bit] + trade(sums[k].astype(BF16), 2 * bit).astype(F32)
        bit *= 2
    frame_grad = back(g, w_frame)
    return (loss.reshape(-1), frame_grad, sums[0] * temper)


def solution(mesh):
    placed = (
        P(("grp", "vid"), None),
        P(),
        P(("grp", "vid"), None),
        P(("grp", "vid")),
        P(("grp", "vid"), None),
        P(("grp", "vid"), None),
        P(("grp", "vid")),
    )
    return jax.shard_map(
        shards,
        mesh=mesh,
        in_specs=placed,
        out_specs=(P(("grp", "vid")), P(("grp", "vid"), None), P(("grp", "vid"), None)),
        check_vma=False,
    )
```

```python
import math

import jax
import jax.numpy as jnp
from jax import lax
from jax.experimental import pallas as pl
from jax.experimental.pallas import tpu as pltpu
from jax.sharding import PartitionSpec as P

F32 = jnp.float32
BF16 = jnp.bfloat16
HIDDEN = -1e30
EMBED_MIB = 52
TILES = 4
PIECES = 4
WIDE = 256
NT = (((1,), (1,)), ((), ()))
TN = (((0,), (0,)), ((), ()))
VMEM = pl.BlockSpec(memory_space=pltpu.VMEM)
SMEM = pl.BlockSpec(memory_space=pltpu.SMEM)
ANYWHERE = pl.BlockSpec(memory_space=pl.ANY)


def params(mib):
    return pltpu.CompilerParams(vmem_limit_bytes=mib * 2**20)


def cost(flops, nbytes, exps=0):
    return pl.CostEstimate(flops=flops, bytes_accessed=nbytes, transcendentals=exps)


def embed_kernel(x_hbm, w_hbm, e_ref, x_ref, w_ref, sem):
    tile = x_ref.shape[0] // TILES
    deep = w_ref.shape[0] // TILES
    reads = []
    for n in range(TILES):
        at = pl.ds(n * deep, deep)
        reads.append(pltpu.make_async_copy(w_hbm.at[at], w_ref.at[at], sem.at[n]))
    for n in range(TILES):
        at = pl.ds(n * tile, tile)
        reads.append(pltpu.make_async_copy(x_hbm.at[at], x_ref.at[at], sem.at[TILES + n]))
    for read in reads:
        read.start()
    for read in reads[:TILES]:
        read.wait()
    for n in range(TILES):
        reads[TILES + n].wait()
        at = slice(n * tile, (n + 1) * tile)
        e_ref[at, :] = jnp.dot(x_ref[at, :], w_ref[...], preferred_element_type=F32).astype(BF16)


def embed(frames, w):
    rows, depth = frames.shape
    width = w.shape[1]
    return pl.pallas_call(
        embed_kernel,
        in_specs=[ANYWHERE, ANYWHERE],
        out_specs=VMEM,
        out_shape=jax.ShapeDtypeStruct((rows, width), BF16),
        scratch_shapes=[
            pltpu.VMEM((rows, depth), BF16),
            pltpu.VMEM((depth, width), BF16),
            pltpu.SemaphoreType.DMA((2 * TILES,)),
        ],
        cost_estimate=cost(2 * rows * depth * width, 2 * (rows * depth + depth * width + rows * width)),
        compiler_params=params(EMBED_MIB),
        name="embed",
    )(frames, w)


def sight_kernel(place_ref, count_ref, tf_ref, ts_ref, keep_ref, give_ref):
    chips, rows = keep_ref.shape
    slots = tf_ref.shape[1]
    line = lax.broadcasted_iota(jnp.int32, (chips, slots), 0)
    slot = lax.broadcasted_iota(jnp.int32, (chips, slots), 1)
    block = lax.broadcasted_iota(jnp.int32, (rows, slots), 0) // 128
    right = jnp.where(tf_ref[...] == block, 1.0, 0.0).astype(BF16)
    for core, out_ref in enumerate((keep_ref, give_ref)):
        video = (2 * line + core) ^ place_ref[0]
        left = jnp.where((ts_ref[...] == video) & (slot < count_ref[0]), 1.0, 0.0).astype(BF16)
        seen = lax.dot_general(left, right, NT, preferred_element_type=F32)
        out_ref[...] = jnp.where(seen > 0.5, 0.0, HIDDEN)


def sight(place, count, tf, ts, chips, rows):
    return pl.pallas_call(
        sight_kernel,
        in_specs=[SMEM, SMEM, VMEM, VMEM],
        out_specs=[VMEM, VMEM],
        out_shape=[jax.ShapeDtypeStruct((chips, rows), F32)] * 2,
        compiler_params=params(24),
        name="sight",
    )(place, count, tf, ts)


def columns(rows):
    for half in range(2):
        for at in range(0, rows, WIDE):
            yield half, slice(at, at + WIDE), slice(half * rows + at, half * rows + at + WIDE)


def score_kernel(ks, temper, *refs):
    n = len(ks)
    es, biases = refs[:2], refs[2:4]
    blocks = refs[4 : 4 + n]
    refs = refs[4 + n :]
    if 0 in ks:
        goal_ref, st_in = refs[0], None
    else:
        st_in = refs[0]
    ps, tops = refs[1 : 1 + n], refs[1 + n : 1 + 2 * n]
    st_ref = refs[1 + 2 * n]
    rows = es[0].shape[0]
    for m, k in enumerate(ks):
        prior = st_in if m == 0 else st_ref
        for half, at, to in columns(rows):
            s = (
                lax.dot_general(blocks[m][...], es[half][at, :], NT, preferred_element_type=F32)
                * temper
            )
            if k == 0 and half == 0:
                hit = goal_ref[:, at] == lax.broadcasted_iota(jnp.int32, s.shape, 0)
                refs[2 + 2 * n][:, at] = jnp.sum(jnp.where(hit, s, 0.0), axis=0, keepdims=True)
            s = s + biases[half][k : k + 1, at]
            top = jnp.max(s, axis=0, keepdims=True)
            if prior is not None:
                top = jnp.maximum(top, prior[0:1, to])
            s = jnp.exp(s - top)
            ps[m][:, to] = s
            total = jnp.sum(s, axis=0, keepdims=True)
            if prior is not None:
                total = total + prior[1:2, to] * jnp.exp(prior[0:1, to] - top)
            tops[m][:, to] = top
            st_ref[0:1, to] = top
            st_ref[1:2, to] = total


def score(ks, temper, es, biases, blocks, last):
    rows, width = es[0].shape
    own = blocks[0].shape[0]
    shapes = [jax.ShapeDtypeStruct((own, 2 * rows), F32)] * len(ks)
    shapes += [jax.ShapeDtypeStruct((1, 2 * rows), F32)] * len(ks)
    shapes += [jax.ShapeDtypeStruct((2, 2 * rows), F32)]
    shapes += [jax.ShapeDtypeStruct((1, rows), F32)] * (0 in ks)
    made = pl.pallas_call(
        lambda *refs: score_kernel(ks, temper, *refs),
        in_specs=[VMEM] * (5 + len(ks)),
        out_specs=[VMEM] * len(shapes),
        out_shape=shapes,
        cost_estimate=cost(
            4 * len(ks) * own * rows * width, 4 * rows * width + 8 * len(ks) * own * rows
        ),
        compiler_params=params(24),
        name=f"score_{ks[-1]}",
    )(*es, *biases, *blocks, last)
    return made[: len(ks)], made[len(ks) : 2 * len(ks)], made[2 * len(ks) :]


def share_kernel(ks, *refs):
    st_ref, got_ref = refs[:2]
    es = refs[2:4]
    n = len(ks)
    ps, tops = refs[4 : 4 + n], refs[4 + n : 4 + 2 * n]
    refs = refs[4 + 2 * n :]
    if 0 in ks:
        goal_ref, pos_ref = refs[:2]
        refs = refs[2:]
    qs, outs = refs[:n], refs[n : 2 * n]
    rows = es[0].shape[0]
    for half in range(2):
        here = slice(half * rows, (half + 1) * rows)
        there = slice((1 - half) * rows, (2 - half) * rows)
        top, other = st_ref[0:1, here], got_ref[0:1, there]
        last = jnp.maximum(top, other)
        total = st_ref[1:2, here] * jnp.exp(top - last) + got_ref[1:2, there] * jnp.exp(other - last)
        if 0 in ks and half == 0:
            refs[2 * n][...] = last + jnp.log(total) - pos_ref[...]
        inverse = 1.0 / total
        for m, k in enumerate(ks):
            scale = jnp.exp(tops[m][:, here] - last) * inverse
            for at in range(0, rows, WIDE):
                to = slice(half * rows + at, half * rows + at + WIDE)
                q = (ps[m][:, to] * scale[:, at : at + WIDE]).astype(BF16)
                if k == 0 and half == 0:
                    hit = goal_ref[:, to] == lax.broadcasted_iota(jnp.int32, q.shape, 0)
                    q = (q.astype(F32) - jnp.where(hit, 1.0, 0.0)).astype(BF16)
                qs[m][:, to] = q
    for m in range(n):
        out = jnp.dot(qs[m][:, :rows], es[0][...], preferred_element_type=F32)
        out = out + jnp.dot(qs[m][:, rows:], es[1][...], preferred_element_type=F32)
        outs[m][...] = out.astype(outs[m].dtype)


def share(ks, kept, st, got, es, *more):
    own, rows2 = kept[ks[0]][0].shape
    width = es[0].shape[1]
    n = len(ks)
    shapes = [jax.ShapeDtypeStruct((own, rows2), BF16)] * n
    shapes += [jax.ShapeDtypeStruct((own, width), BF16 if k % 2 else F32) for k in ks]
    shapes += [jax.ShapeDtypeStruct((1, rows2 // 2), F32)] * (0 in ks)
    made = pl.pallas_call(
        lambda *refs: share_kernel(ks, *refs),
        in_specs=[VMEM] * (4 + 2 * n + len(more)),
        out_specs=[VMEM] * len(shapes),
        out_shape=shapes,
        cost_estimate=cost(2 * n * own * rows2 * width, n * 6 * own * rows2 + 2 * rows2 * width),
        compiler_params=params(40),
        name=f"share_{ks[0]}",
    )(st, got, *es, *[kept[k][0] for k in ks], *[kept[k][1] for k in ks], *more)
    return made[:n], made[n : 2 * n], made[2 * n :]


def part_rows(qs, table, at):
    q = jnp.concatenate([q_ref[:, at] for q_ref in qs], axis=0)
    return lax.dot_general(q, table, TN, preferred_element_type=F32)


def rows_kernel(n, first, *refs):
    table = jnp.concatenate([ref[...] for ref in refs[n : 2 * n]], axis=0)
    for turn, out_ref in enumerate(refs[2 * n :]):
        base = first + turn * out_ref.shape[0]
        for at in range(0, out_ref.shape[0], WIDE):
            part = part_rows(refs[:n], table, slice(base + at, base + at + WIDE))
            out_ref[at : at + WIDE, :] = part.astype(out_ref.dtype)


def rows_of(qs, blocks, theirs):
    n = len(qs)
    own, rows2 = qs[0].shape
    rows, width = rows2 // 2, blocks[0].shape[1]
    cut = PIECES if theirs else 1
    shape = jax.ShapeDtypeStruct((rows // cut, width), BF16 if theirs else F32)
    return pl.pallas_call(
        lambda *refs: rows_kernel(n, rows if theirs else 0, *refs),
        in_specs=[VMEM] * (2 * n),
        out_specs=[VMEM] * cut,
        out_shape=[shape] * cut,
        cost_estimate=cost(n * own * rows2 * width, 2 * n * own * (rows2 + width)),
        compiler_params=params(24),
        name="rows_theirs" if theirs else "rows_mine",
    )(*qs, *blocks)


def back_kernel(temper, mine_ref, w_ref, *refs):
    *gots, out_hbm, out_ref, sem = refs
    size = gots[0].shape[0]
    writes = []
    for turn, at in enumerate(range(0, out_ref.shape[0], WIDE)):
        cut = slice(at, at + WIDE)
        inner = slice(at % size, at % size + WIDE)
        g = (mine_ref[cut, :] + gots[at // size][inner, :].astype(F32)) * temper
        out_ref[cut, :] = lax.dot_general(
            g.astype(BF16), w_ref[...], NT, preferred_element_type=F32
        ).astype(BF16)
        cut = pl.ds(at, WIDE)
        writes.append(pltpu.make_async_copy(out_ref.at[cut], out_hbm.at[cut], sem.at[turn]))
        writes[-1].start()
    for write in writes:
        write.wait()


def back(mine, gots, w, temper):
    rows, width = mine.shape
    depth = w.shape[0]
    return pl.pallas_call(
        lambda *refs: back_kernel(temper, *refs),
        in_specs=[VMEM] * (2 + len(gots)),
        out_specs=ANYWHERE,
        out_shape=jax.ShapeDtypeStruct((rows, depth), BF16),
        scratch_shapes=[
            pltpu.VMEM((rows, depth), BF16),
            pltpu.SemaphoreType.DMA((rows // WIDE,)),
        ],
        cost_estimate=cost(2 * rows * width * depth, 2 * (depth * width + rows * depth)),
        compiler_params=params(40),
        name="back",
    )(mine, w, *gots)


def shards(frames, w_frame, step_emb, targets, tile_frame, tile_step, tile_count):
    videos = lax.axis_size("vid")
    chips = videos // 2
    rows = frames.shape[0]
    temper = 1.0 / math.sqrt(step_emb.shape[1])
    place = lax.axis_index("vid").astype(jnp.int32).reshape(1)
    goals = targets.reshape(1, -1)

    def trade(x, k):
        return lax.ppermute(x, "vid", [(i, i ^ k) for i in range(videos)])

    order, bit = [0], chips // 2
    while bit:
        order += [k ^ bit for k in order]
        bit //= 2
    e = embed(frames, w_frame)
    keep, lend = sight(place, tile_count, tile_frame, tile_step, chips, rows)
    biases = (keep, trade(lend, 1))
    mine, kept, st = {0: step_emb}, {}, goals
    for ks in [tuple(order[:2])] + [(k,) for k in order[2:]]:
        k = ks[-1]
        low = k & -k
        if 0 in ks:
            near = trade(step_emb, 2)
            come = trade(step_emb, 2 * low)
            mine[1], mine[k], e = lax.optimization_barrier((near, come, e))
            es = (e, trade(e, 1))
        elif k > 1:
            come = trade(mine[k ^ low], 2 * low)
            mine[k], gate = lax.optimization_barrier((come, st))
        ps, tops, (st, *pos) = score(ks, temper, es, biases, [mine[m] for m in ks], st)
        if pos:
            found = pos[0]
        for m, p, top in zip(ks, ps, tops):
            kept[m] = (p, top)
    got = trade(st, 1)

    qs, sums = {}, {}
    for ks in [(k,) for k in range(chips - 1, 2, -1)] + [(2, 1, 0)]:
        more = (goals, found) if 0 in ks else ()
        made, parts, loss = share(ks, kept, st, got, es, *more)
        qs.update(zip(ks, made))
        sums.update(zip(ks, parts))
        if 0 not in ks:
            e, qs[ks[0]] = lax.optimization_barrier((es[0], qs[ks[0]]))
            es = (e, es[1])
    parts = [qs[k] for k in order], [mine[k] for k in order]
    lent = [trade(piece, 1) for piece in rows_of(*parts, True)]
    (own_rows,) = rows_of(*parts, False)
    sums[1], own_rows = lax.optimization_barrier((sums[1], own_rows))
    frame_grad = back(own_rows, lent, w_frame, temper)
    bit = 1
    while bit < chips:
        for k in range(chips - bit, 0, -2 * bit):
            come = trade(sums[k].astype(BF16), 2 * bit)
            if 2 * bit == chips:
                come, frame_grad = lax.optimization_barrier((come, frame_grad))
            sums[k - bit] = sums[k - bit].astype(F32) + come.astype(F32)
        bit *= 2
    return (loss[0].reshape(-1), frame_grad, sums[0] * temper)


def solution(mesh):
    placed = (
        P(("grp", "vid"), None),
        P(),
        P(("grp", "vid"), None),
        P(("grp", "vid")),
        P(("grp", "vid"), None),
        P(("grp", "vid"), None),
        P(("grp", "vid")),
    )
    return jax.shard_map(
        shards,
        mesh=mesh,
        in_specs=placed,
        out_specs=(P(("grp", "vid")), P(("grp", "vid"), None), P(("grp", "vid"), None)),
        check_vma=False,
    )
```

```python
import math

import jax
import jax.numpy as jnp
from jax import lax
from jax.experimental import pallas as pl
from jax.experimental.pallas import tpu as pltpu
from jax.sharding import PartitionSpec as P

F32 = jnp.float32
BF16 = jnp.bfloat16
HIDDEN = -1e30
EMBED_MIB = 52
TILES = 4
PIECES = 4
WIDE = 256
NT = (((1,), (1,)), ((), ()))
TN = (((0,), (0,)), ((), ()))
VMEM = pl.BlockSpec(memory_space=pltpu.VMEM)
SMEM = pl.BlockSpec(memory_space=pltpu.SMEM)
ANYWHERE = pl.BlockSpec(memory_space=pl.ANY)


def params(mib):
    return pltpu.CompilerParams(vmem_limit_bytes=mib * 2**20)


def cost(flops, nbytes, exps=0):
    return pl.CostEstimate(flops=flops, bytes_accessed=nbytes, transcendentals=exps)


def embed_kernel(x_hbm, w_hbm, e_ref, x_ref, w_ref, sem):
    tile = x_ref.shape[0] // TILES
    deep = w_ref.shape[0] // TILES
    reads = []
    for n in range(TILES):
        at = pl.ds(n * deep, deep)
        reads.append(pltpu.make_async_copy(w_hbm.at[at], w_ref.at[at], sem.at[n]))
    for n in range(TILES):
        at = pl.ds(n * tile, tile)
        reads.append(pltpu.make_async_copy(x_hbm.at[at], x_ref.at[at], sem.at[TILES + n]))
    for read in reads:
        read.start()
    for read in reads[:TILES]:
        read.wait()
    for n in range(TILES):
        reads[TILES + n].wait()
        at = slice(n * tile, (n + 1) * tile)
        e_ref[at, :] = jnp.dot(x_ref[at, :], w_ref[...], preferred_element_type=F32).astype(BF16)


def embed(frames, w):
    rows, depth = frames.shape
    width = w.shape[1]
    return pl.pallas_call(
        embed_kernel,
        in_specs=[ANYWHERE, ANYWHERE],
        out_specs=VMEM,
        out_shape=jax.ShapeDtypeStruct((rows, width), BF16),
        scratch_shapes=[
            pltpu.VMEM((rows, depth), BF16),
            pltpu.VMEM((depth, width), BF16),
            pltpu.SemaphoreType.DMA((2 * TILES,)),
        ],
        cost_estimate=cost(2 * rows * depth * width, 2 * (rows * depth + depth * width + rows * width)),
        compiler_params=params(EMBED_MIB),
        name="embed",
    )(frames, w)


def sight_kernel(place_ref, count_ref, tf_ref, ts_ref, keep_ref, give_ref):
    chips, rows = keep_ref.shape
    slots = tf_ref.shape[1]
    line = lax.broadcasted_iota(jnp.int32, (chips, slots), 0)
    slot = lax.broadcasted_iota(jnp.int32, (chips, slots), 1)
    block = lax.broadcasted_iota(jnp.int32, (rows, slots), 0) // 128
    right = jnp.where(tf_ref[...] == block, 1.0, 0.0).astype(BF16)
    for core, out_ref in enumerate((keep_ref, give_ref)):
        video = (2 * line + core) ^ place_ref[0]
        left = jnp.where((ts_ref[...] == video) & (slot < count_ref[0]), 1.0, 0.0).astype(BF16)
        seen = lax.dot_general(left, right, NT, preferred_element_type=F32)
        out_ref[...] = jnp.where(seen > 0.5, 0.0, HIDDEN)


def sight(place, count, tf, ts, chips, rows):
    return pl.pallas_call(
        sight_kernel,
        in_specs=[SMEM, SMEM, VMEM, VMEM],
        out_specs=[VMEM, VMEM],
        out_shape=[jax.ShapeDtypeStruct((chips, rows), F32)] * 2,
        compiler_params=params(24),
        name="sight",
    )(place, count, tf, ts)


def columns(rows):
    for half in range(2):
        for at in range(0, rows, WIDE):
            yield half, slice(at, at + WIDE), slice(half * rows + at, half * rows + at + WIDE)


def score_kernel(ks, temper, *refs):
    n = len(ks)
    es, biases = refs[:2], refs[2:4]
    blocks = refs[4 : 4 + n]
    refs = refs[4 + n :]
    if 0 in ks:
        goal_ref, st_in = refs[0], None
    else:
        st_in = refs[0]
    ps, top_ref, st_ref = refs[1 : 1 + n], refs[1 + n], refs[2 + n]
    rows, own = es[0].shape[0], blocks[0].shape[0]
    table = blocks[0][...] if n == 1 else jnp.concatenate([ref[...] for ref in blocks], axis=0)
    for half, at, to in columns(rows):
        s = lax.dot_general(table, es[half][at, :], NT, preferred_element_type=F32) * temper
        cuts = [s[m * own : (m + 1) * own] for m in range(n)]
        if 0 in ks and half == 0:
            hit = goal_ref[:, at] == lax.broadcasted_iota(jnp.int32, (own, WIDE), 0)
            found = jnp.sum(jnp.where(hit, cuts[ks.index(0)], 0.0), axis=0, keepdims=True)
            refs[3 + n][:, at] = found
        top = None if st_in is None else st_in[0:1, to]
        for m, k in enumerate(ks):
            cuts[m] = cuts[m] + biases[half][k : k + 1, at]
            high = jnp.max(cuts[m], axis=0, keepdims=True)
            top = high if top is None else jnp.maximum(top, high)
        total = None if st_in is None else st_in[1:2, to] * jnp.exp(st_in[0:1, to] - top)
        for m in range(n):
            p = jnp.exp(cuts[m] - top)
            ps[m][:, to] = p
            part = jnp.sum(p, axis=0, keepdims=True)
            total = part if total is None else total + part
        top_ref[:, to] = top
        st_ref[0:1, to] = top
        st_ref[1:2, to] = total


def score(ks, temper, es, biases, blocks, last):
    rows, width = es[0].shape
    own = blocks[0].shape[0]
    shapes = [jax.ShapeDtypeStruct((own, 2 * rows), F32)] * len(ks)
    shapes += [jax.ShapeDtypeStruct((1, 2 * rows), F32)]
    shapes += [jax.ShapeDtypeStruct((2, 2 * rows), F32)]
    shapes += [jax.ShapeDtypeStruct((1, rows), F32)] * (0 in ks)
    made = pl.pallas_call(
        lambda *refs: score_kernel(ks, temper, *refs),
        in_specs=[VMEM] * (5 + len(ks)),
        out_specs=[VMEM] * len(shapes),
        out_shape=shapes,
        cost_estimate=cost(
            4 * len(ks) * own * rows * width, 4 * rows * width + 8 * len(ks) * own * rows
        ),
        compiler_params=params(24),
        name=f"score_{ks[-1]}",
    )(*es, *biases, *blocks, last)
    return made[: len(ks)], made[len(ks)], made[len(ks) + 1 :]


def share_kernel(ks, *refs):
    st_ref, got_ref = refs[:2]
    es = refs[2:4]
    n = len(ks)
    ps, tops = refs[4 : 4 + n], refs[4 + n : 4 + 2 * n]
    refs = refs[4 + 2 * n :]
    if 0 in ks:
        goal_ref, pos_ref = refs[:2]
        refs = refs[2:]
    qs, outs = refs[:n], refs[n : 2 * n]
    rows = es[0].shape[0]
    for half in range(2):
        here = slice(half * rows, (half + 1) * rows)
        there = slice((1 - half) * rows, (2 - half) * rows)
        top, other = st_ref[0:1, here], got_ref[0:1, there]
        last = jnp.maximum(top, other)
        total = st_ref[1:2, here] * jnp.exp(top - last) + got_ref[1:2, there] * jnp.exp(other - last)
        if 0 in ks and half == 0:
            refs[2 * n][...] = last + jnp.log(total) - pos_ref[...]
        inverse = 1.0 / total
        for m, k in enumerate(ks):
            scale = jnp.exp(tops[m][:, here] - last) * inverse
            for at in range(0, rows, WIDE):
                to = slice(half * rows + at, half * rows + at + WIDE)
                q = (ps[m][:, to] * scale[:, at : at + WIDE]).astype(BF16)
                if k == 0 and half == 0:
                    hit = goal_ref[:, to] == lax.broadcasted_iota(jnp.int32, q.shape, 0)
                    q = (q.astype(F32) - jnp.where(hit, 1.0, 0.0)).astype(BF16)
                qs[m][:, to] = q
    for m in range(n):
        out = jnp.dot(qs[m][:, :rows], es[0][...], preferred_element_type=F32)
        out = out + jnp.dot(qs[m][:, rows:], es[1][...], preferred_element_type=F32)
        outs[m][...] = out.astype(outs[m].dtype)


def share(ks, kept, st, got, es, *more):
    own, rows2 = kept[ks[0]][0].shape
    width = es[0].shape[1]
    n = len(ks)
    shapes = [jax.ShapeDtypeStruct((own, rows2), BF16)] * n
    shapes += [jax.ShapeDtypeStruct((own, width), BF16 if k % 2 else F32) for k in ks]
    shapes += [jax.ShapeDtypeStruct((1, rows2 // 2), F32)] * (0 in ks)
    made = pl.pallas_call(
        lambda *refs: share_kernel(ks, *refs),
        in_specs=[VMEM] * (4 + 2 * n + len(more)),
        out_specs=[VMEM] * len(shapes),
        out_shape=shapes,
        cost_estimate=cost(2 * n * own * rows2 * width, n * 6 * own * rows2 + 2 * rows2 * width),
        compiler_params=params(40),
        name=f"share_{ks[0]}",
    )(st, got, *es, *[kept[k][0] for k in ks], *[kept[k][1] for k in ks], *more)
    return made[:n], made[n : 2 * n], made[2 * n :]


def part_rows(qs, table, at):
    q = jnp.concatenate([q_ref[:, at] for q_ref in qs], axis=0)
    return lax.dot_general(q, table, TN, preferred_element_type=F32)


def rows_kernel(n, first, *refs):
    table = jnp.concatenate([ref[...] for ref in refs[n : 2 * n]], axis=0)
    for turn, out_ref in enumerate(refs[2 * n :]):
        base = first + turn * out_ref.shape[0]
        for at in range(0, out_ref.shape[0], WIDE):
            part = part_rows(refs[:n], table, slice(base + at, base + at + WIDE))
            out_ref[at : at + WIDE, :] = part.astype(out_ref.dtype)


def rows_of(qs, blocks, theirs):
    n = len(qs)
    own, rows2 = qs[0].shape
    rows, width = rows2 // 2, blocks[0].shape[1]
    cut = PIECES if theirs else 1
    shape = jax.ShapeDtypeStruct((rows // cut, width), BF16 if theirs else F32)
    return pl.pallas_call(
        lambda *refs: rows_kernel(n, rows if theirs else 0, *refs),
        in_specs=[VMEM] * (2 * n),
        out_specs=[VMEM] * cut,
        out_shape=[shape] * cut,
        cost_estimate=cost(n * own * rows2 * width, 2 * n * own * (rows2 + width)),
        compiler_params=params(24),
        name="rows_theirs" if theirs else "rows_mine",
    )(*qs, *blocks)


def back_kernel(temper, mine_ref, w_ref, *refs):
    *gots, out_hbm, out_ref, sem = refs
    size = gots[0].shape[0]
    writes = []
    for turn, at in enumerate(range(0, out_ref.shape[0], WIDE)):
        cut = slice(at, at + WIDE)
        inner = slice(at % size, at % size + WIDE)
        g = (mine_ref[cut, :] + gots[at // size][inner, :].astype(F32)) * temper
        out_ref[cut, :] = lax.dot_general(
            g.astype(BF16), w_ref[...], NT, preferred_element_type=F32
        ).astype(BF16)
        cut = pl.ds(at, WIDE)
        writes.append(pltpu.make_async_copy(out_ref.at[cut], out_hbm.at[cut], sem.at[turn]))
        writes[-1].start()
    for write in writes:
        write.wait()


def back(mine, gots, w, temper):
    rows, width = mine.shape
    depth = w.shape[0]
    return pl.pallas_call(
        lambda *refs: back_kernel(temper, *refs),
        in_specs=[VMEM] * (2 + len(gots)),
        out_specs=ANYWHERE,
        out_shape=jax.ShapeDtypeStruct((rows, depth), BF16),
        scratch_shapes=[
            pltpu.VMEM((rows, depth), BF16),
            pltpu.SemaphoreType.DMA((rows // WIDE,)),
        ],
        cost_estimate=cost(2 * rows * width * depth, 2 * (depth * width + rows * depth)),
        compiler_params=params(40),
        name="back",
    )(mine, w, *gots)


def shards(frames, w_frame, step_emb, targets, tile_frame, tile_step, tile_count):
    videos = lax.axis_size("vid")
    chips = videos // 2
    rows = frames.shape[0]
    temper = 1.0 / math.sqrt(step_emb.shape[1])
    place = lax.axis_index("vid").astype(jnp.int32).reshape(1)
    goals = targets.reshape(1, -1)

    def trade(x, k):
        return lax.ppermute(x, "vid", [(i, i ^ k) for i in range(videos)])

    order, bit = [0], chips // 2
    while bit:
        order += [k ^ bit for k in order]
        bit //= 2
    e = embed(frames, w_frame)
    keep, lend = sight(place, tile_count, tile_frame, tile_step, chips, rows)
    biases = (keep, trade(lend, 1))
    mine, kept, st = {0: step_emb}, {}, goals
    near = trade(step_emb, 2)
    far = chips // 2
    come = trade(step_emb, 2 * far)
    mine[1], mine[far], e = lax.optimization_barrier((near, come, e))
    es = (e, trade(e, 1))
    early = (0, far, 1)
    for ks in [early] + [(k,) for k in order if k not in early]:
        k = ks[0]
        if k > 0:
            low = k & -k
            come = trade(mine[k ^ low], 2 * low)
            mine[k], gate = lax.optimization_barrier((come, st))
        ps, top, (st, *pos) = score(ks, temper, es, biases, [mine[m] for m in ks], st)
        if pos:
            found = pos[0]
        for m, p in zip(ks, ps):
            kept[m] = (p, top)
    got = trade(st, 1)

    qs, sums = {}, {}
    for ks in [(k,) for k in range(chips - 1, 2, -1)] + [(2, 1, 0)]:
        more = (goals, found) if 0 in ks else ()
        made, parts, loss = share(ks, kept, st, got, es, *more)
        qs.update(zip(ks, made))
        sums.update(zip(ks, parts))
        if 0 not in ks:
            e, qs[ks[0]] = lax.optimization_barrier((es[0], qs[ks[0]]))
            es = (e, es[1])
    parts = [qs[k] for k in order], [mine[k] for k in order]
    lent = [trade(piece, 1) for piece in rows_of(*parts, True)]
    (own_rows,) = rows_of(*parts, False)
    sums[1], own_rows = lax.optimization_barrier((sums[1], own_rows))
    frame_grad = back(own_rows, lent, w_frame, temper)
    bit = 1
    while bit < chips:
        for k in range(chips - bit, 0, -2 * bit):
            come = trade(sums[k].astype(BF16), 2 * bit)
            if 2 * bit == chips:
                come, frame_grad = lax.optimization_barrier((come, frame_grad))
            sums[k - bit] = sums[k - bit].astype(F32) + come.astype(F32)
        bit *= 2
    return (loss[0].reshape(-1), frame_grad, sums[0] * temper)


def solution(mesh):
    placed = (
        P(("grp", "vid"), None),
        P(),
        P(("grp", "vid"), None),
        P(("grp", "vid")),
        P(("grp", "vid"), None),
        P(("grp", "vid"), None),
        P(("grp", "vid")),
    )
    return jax.shard_map(
        shards,
        mesh=mesh,
        in_specs=placed,
        out_specs=(P(("grp", "vid")), P(("grp", "vid"), None), P(("grp", "vid"), None)),
        check_vma=False,
    )
```

```python
import math

import jax
import jax.numpy as jnp
from jax import lax
from jax.experimental import pallas as pl
from jax.experimental.pallas import tpu as pltpu
from jax.sharding import PartitionSpec as P

F32 = jnp.float32
BF16 = jnp.bfloat16
HIDDEN = -1e30
EMBED_MIB = 52
TILES = 4
PIECES = 4
WIDE = 256
NT = (((1,), (1,)), ((), ()))
TN = (((0,), (0,)), ((), ()))
VMEM = pl.BlockSpec(memory_space=pltpu.VMEM)
SMEM = pl.BlockSpec(memory_space=pltpu.SMEM)
ANYWHERE = pl.BlockSpec(memory_space=pl.ANY)


def params(mib):
    return pltpu.CompilerParams(vmem_limit_bytes=mib * 2**20)


def cost(flops, nbytes, exps=0):
    return pl.CostEstimate(flops=flops, bytes_accessed=nbytes, transcendentals=exps)


def embed_kernel(x_hbm, w_hbm, e_ref, x_ref, w_ref, sem):
    tile = x_ref.shape[0] // TILES
    deep = w_ref.shape[0] // TILES
    reads = []
    for n in range(TILES):
        at = pl.ds(n * deep, deep)
        reads.append(pltpu.make_async_copy(w_hbm.at[at], w_ref.at[at], sem.at[n]))
    for n in range(TILES):
        at = pl.ds(n * tile, tile)
        reads.append(pltpu.make_async_copy(x_hbm.at[at], x_ref.at[at], sem.at[TILES + n]))
    for read in reads:
        read.start()
    for read in reads[:TILES]:
        read.wait()
    for n in range(TILES):
        reads[TILES + n].wait()
        at = slice(n * tile, (n + 1) * tile)
        e_ref[at, :] = jnp.dot(x_ref[at, :], w_ref[...], preferred_element_type=F32).astype(BF16)


def embed(frames, w):
    rows, depth = frames.shape
    width = w.shape[1]
    return pl.pallas_call(
        embed_kernel,
        in_specs=[ANYWHERE, ANYWHERE],
        out_specs=VMEM,
        out_shape=jax.ShapeDtypeStruct((rows, width), BF16),
        scratch_shapes=[
            pltpu.VMEM((rows, depth), BF16),
            pltpu.VMEM((depth, width), BF16),
            pltpu.SemaphoreType.DMA((2 * TILES,)),
        ],
        cost_estimate=cost(2 * rows * depth * width, 2 * (rows * depth + depth * width + rows * width)),
        compiler_params=params(EMBED_MIB),
        name="embed",
    )(frames, w)


def sight_kernel(place_ref, count_ref, tf_ref, ts_ref, keep_ref, give_ref):
    chips, rows = keep_ref.shape
    slots = tf_ref.shape[1]
    line = lax.broadcasted_iota(jnp.int32, (chips, slots), 0)
    slot = lax.broadcasted_iota(jnp.int32, (chips, slots), 1)
    block = lax.broadcasted_iota(jnp.int32, (rows, slots), 0) // 128
    right = jnp.where(tf_ref[...] == block, 1.0, 0.0).astype(BF16)
    for core, out_ref in enumerate((keep_ref, give_ref)):
        video = (2 * line + core) ^ place_ref[0]
        left = jnp.where((ts_ref[...] == video) & (slot < count_ref[0]), 1.0, 0.0).astype(BF16)
        seen = lax.dot_general(left, right, NT, preferred_element_type=F32)
        out_ref[...] = jnp.where(seen > 0.5, 0.0, HIDDEN)


def sight(place, count, tf, ts, chips, rows):
    return pl.pallas_call(
        sight_kernel,
        in_specs=[SMEM, SMEM, VMEM, VMEM],
        out_specs=[VMEM, VMEM],
        out_shape=[jax.ShapeDtypeStruct((chips, rows), F32)] * 2,
        compiler_params=params(24),
        name="sight",
    )(place, count, tf, ts)


def columns(rows):
    for half in range(2):
        for at in range(0, rows, WIDE):
            yield half, slice(at, at + WIDE), slice(half * rows + at, half * rows + at + WIDE)


def score_kernel(ks, temper, *refs):
    n = len(ks)
    es, biases = refs[:2], refs[2:4]
    blocks = refs[4 : 4 + n]
    refs = refs[4 + n :]
    if 0 in ks:
        goal_ref, st_in = refs[0], None
    else:
        st_in = refs[0]
    ps, top_ref, st_ref = refs[1 : 1 + n], refs[1 + n], refs[2 + n]
    rows, own = es[0].shape[0], blocks[0].shape[0]
    table = blocks[0][...] if n == 1 else jnp.concatenate([ref[...] for ref in blocks], axis=0)
    for half, at, to in columns(rows):
        s = lax.dot_general(table, es[half][at, :], NT, preferred_element_type=F32) * temper
        cuts = [s[m * own : (m + 1) * own] for m in range(n)]
        if 0 in ks and half == 0:
            hit = goal_ref[:, at] == lax.broadcasted_iota(jnp.int32, (own, WIDE), 0)
            found = jnp.sum(jnp.where(hit, cuts[ks.index(0)], 0.0), axis=0, keepdims=True)
            refs[3 + n][:, at] = found
        top = None if st_in is None else st_in[0:1, to]
        for m, k in enumerate(ks):
            cuts[m] = cuts[m] + biases[half][k : k + 1, at]
            high = jnp.max(cuts[m], axis=0, keepdims=True)
            top = high if top is None else jnp.maximum(top, high)
        total = None if st_in is None else st_in[1:2, to] * jnp.exp(st_in[0:1, to] - top)
        for m in range(n):
            p = jnp.exp(cuts[m] - top)
            ps[m][:, to] = p
            part = jnp.sum(p, axis=0, keepdims=True)
            total = part if total is None else total + part
        top_ref[:, to] = top
        st_ref[0:1, to] = top
        st_ref[1:2, to] = total


def score(ks, temper, es, biases, blocks, last):
    rows, width = es[0].shape
    own = blocks[0].shape[0]
    shapes = [jax.ShapeDtypeStruct((own, 2 * rows), F32)] * len(ks)
    shapes += [jax.ShapeDtypeStruct((1, 2 * rows), F32)]
    shapes += [jax.ShapeDtypeStruct((2, 2 * rows), F32)]
    shapes += [jax.ShapeDtypeStruct((1, rows), F32)] * (0 in ks)
    made = pl.pallas_call(
        lambda *refs: score_kernel(ks, temper, *refs),
        in_specs=[VMEM] * (5 + len(ks)),
        out_specs=[VMEM] * len(shapes),
        out_shape=shapes,
        cost_estimate=cost(
            4 * len(ks) * own * rows * width, 4 * rows * width + 8 * len(ks) * own * rows
        ),
        compiler_params=params(24),
        name=f"score_{ks[-1]}",
    )(*es, *biases, *blocks, last)
    return made[: len(ks)], made[len(ks)], made[len(ks) + 1 :]


def share_kernel(ks, *refs):
    st_ref, got_ref = refs[:2]
    es = refs[2:4]
    n = len(ks)
    ps, tops = refs[4 : 4 + n], refs[4 + n : 4 + 2 * n]
    refs = refs[4 + 2 * n :]
    if 0 in ks:
        goal_ref, pos_ref = refs[:2]
        refs = refs[2:]
    qs, outs = refs[:n], refs[n : 2 * n]
    rows = es[0].shape[0]
    for half in range(2):
        here = slice(half * rows, (half + 1) * rows)
        there = slice((1 - half) * rows, (2 - half) * rows)
        top, other = st_ref[0:1, here], got_ref[0:1, there]
        last = jnp.maximum(top, other)
        total = st_ref[1:2, here] * jnp.exp(top - last) + got_ref[1:2, there] * jnp.exp(other - last)
        if 0 in ks and half == 0:
            refs[2 * n][...] = last + jnp.log(total) - pos_ref[...]
        inverse = 1.0 / total
        for m, k in enumerate(ks):
            scale = jnp.exp(tops[m][:, here] - last) * inverse
            for at in range(0, rows, WIDE):
                to = slice(half * rows + at, half * rows + at + WIDE)
                q = (ps[m][:, to] * scale[:, at : at + WIDE]).astype(BF16)
                if k == 0 and half == 0:
                    hit = goal_ref[:, to] == lax.broadcasted_iota(jnp.int32, q.shape, 0)
                    q = (q.astype(F32) - jnp.where(hit, 1.0, 0.0)).astype(BF16)
                qs[m][:, to] = q
    for m in range(n):
        out = jnp.dot(qs[m][:, :rows], es[0][...], preferred_element_type=F32)
        out = out + jnp.dot(qs[m][:, rows:], es[1][...], preferred_element_type=F32)
        outs[m][...] = out.astype(outs[m].dtype)


def share(ks, kept, st, got, es, *more):
    own, rows2 = kept[ks[0]][0].shape
    width = es[0].shape[1]
    n = len(ks)
    shapes = [jax.ShapeDtypeStruct((own, rows2), BF16)] * n
    shapes += [jax.ShapeDtypeStruct((own, width), BF16 if k % 2 else F32) for k in ks]
    shapes += [jax.ShapeDtypeStruct((1, rows2 // 2), F32)] * (0 in ks)
    made = pl.pallas_call(
        lambda *refs: share_kernel(ks, *refs),
        in_specs=[VMEM] * (4 + 2 * n + len(more)),
        out_specs=[VMEM] * len(shapes),
        out_shape=shapes,
        cost_estimate=cost(2 * n * own * rows2 * width, n * 6 * own * rows2 + 2 * rows2 * width),
        compiler_params=params(40),
        name=f"share_{ks[0]}",
    )(st, got, *es, *[kept[k][0] for k in ks], *[kept[k][1] for k in ks], *more)
    return made[:n], made[n : 2 * n], made[2 * n :]


def part_rows(qs, table, at):
    q = jnp.concatenate([q_ref[:, at] for q_ref in qs], axis=0)
    return lax.dot_general(q, table, TN, preferred_element_type=F32)


def rows_kernel(n, first, *refs):
    table = jnp.concatenate([ref[...] for ref in refs[n : 2 * n]], axis=0)
    for turn, out_ref in enumerate(refs[2 * n :]):
        base = first + turn * out_ref.shape[0]
        for at in range(0, out_ref.shape[0], WIDE):
            part = part_rows(refs[:n], table, slice(base + at, base + at + WIDE))
            out_ref[at : at + WIDE, :] = part.astype(out_ref.dtype)


def rows_of(qs, blocks, theirs):
    n = len(qs)
    own, rows2 = qs[0].shape
    rows, width = rows2 // 2, blocks[0].shape[1]
    cut = PIECES if theirs else 1
    shape = jax.ShapeDtypeStruct((rows // cut, width), BF16 if theirs else F32)
    return pl.pallas_call(
        lambda *refs: rows_kernel(n, rows if theirs else 0, *refs),
        in_specs=[VMEM] * (2 * n),
        out_specs=[VMEM] * cut,
        out_shape=[shape] * cut,
        cost_estimate=cost(n * own * rows2 * width, 2 * n * own * (rows2 + width)),
        compiler_params=params(24),
        name="rows_theirs" if theirs else "rows_mine",
    )(*qs, *blocks)


def back_kernel(temper, mine_ref, w_ref, *refs):
    *gots, out_hbm, out_ref, sem = refs
    size = gots[0].shape[0]
    writes = []
    for turn, at in enumerate(range(0, out_ref.shape[0], WIDE)):
        cut = slice(at, at + WIDE)
        inner = slice(at % size, at % size + WIDE)
        g = (mine_ref[cut, :] + gots[at // size][inner, :].astype(F32)) * temper
        out_ref[cut, :] = lax.dot_general(
            g.astype(BF16), w_ref[...], NT, preferred_element_type=F32
        ).astype(BF16)
        cut = pl.ds(at, WIDE)
        writes.append(pltpu.make_async_copy(out_ref.at[cut], out_hbm.at[cut], sem.at[turn]))
        writes[-1].start()
    for write in writes:
        write.wait()


def back(mine, gots, w, temper):
    rows, width = mine.shape
    depth = w.shape[0]
    return pl.pallas_call(
        lambda *refs: back_kernel(temper, *refs),
        in_specs=[VMEM] * (2 + len(gots)),
        out_specs=ANYWHERE,
        out_shape=jax.ShapeDtypeStruct((rows, depth), BF16),
        scratch_shapes=[
            pltpu.VMEM((rows, depth), BF16),
            pltpu.SemaphoreType.DMA((rows // WIDE,)),
        ],
        cost_estimate=cost(2 * rows * width * depth, 2 * (depth * width + rows * depth)),
        compiler_params=params(40),
        name="back",
    )(mine, w, *gots)


def shards(frames, w_frame, step_emb, targets, tile_frame, tile_step, tile_count):
    videos = lax.axis_size("vid")
    chips = videos // 2
    rows = frames.shape[0]
    temper = 1.0 / math.sqrt(step_emb.shape[1])
    place = lax.axis_index("vid").astype(jnp.int32).reshape(1)
    goals = targets.reshape(1, -1)

    def trade(x, k):
        return lax.ppermute(x, "vid", [(i, i ^ k) for i in range(videos)])

    order, bit = [0], chips // 2
    while bit:
        order += [k ^ bit for k in order]
        bit //= 2
    e = embed(frames, w_frame)
    keep, lend = sight(place, tile_count, tile_frame, tile_step, chips, rows)
    biases = (keep, trade(lend, 1))
    mine, kept, st = {0: step_emb}, {}, goals
    near = trade(step_emb, 2)
    far = chips // 2
    come = trade(step_emb, 2 * far)
    mine[1], mine[far], e = lax.optimization_barrier((near, come, e))
    es = (e, trade(e, 1))
    early = (0, far, 1)
    for ks in [early] + [(k,) for k in order if k not in early]:
        k = ks[0]
        if k > 0:
            low = k & -k
            come = trade(mine[k ^ low], 2 * low)
            mine[k], gate = lax.optimization_barrier((come, st))
        ps, top, (st, *pos) = score(ks, temper, es, biases, [mine[m] for m in ks], st)
        if pos:
            found = pos[0]
        for m, p in zip(ks, ps):
            kept[m] = (p, top)
    got = trade(st, 1)

    qs, sums = {}, {}
    for ks in [(k,) for k in range(chips - 1, 2, -1)] + [(2, 1, 0)]:
        more = (goals, found) if 0 in ks else ()
        made, parts, loss = share(ks, kept, st, got, es, *more)
        qs.update(zip(ks, made))
        sums.update(zip(ks, parts))
        if 0 not in ks:
            e, qs[ks[0]] = lax.optimization_barrier((es[0], qs[ks[0]]))
            es = (e, es[1])
    parts = [qs[k] for k in order], [mine[k] for k in order]
    lent = [trade(piece, 1) for piece in rows_of(*parts, True)]
    (own_rows,) = rows_of(*parts, False)
    frame_grad = back(own_rows, lent, w_frame, temper)
    bit = 1
    while bit < chips:
        for k in range(chips - bit, 0, -2 * bit):
            come = trade(sums[k].astype(BF16), 2 * bit)
            if 2 * bit == chips:
                come, frame_grad = lax.optimization_barrier((come, frame_grad))
            sums[k - bit] = sums[k - bit].astype(F32) + come.astype(F32)
        bit *= 2
    return (loss[0].reshape(-1), frame_grad, sums[0] * temper)


def solution(mesh):
    placed = (
        P(("grp", "vid"), None),
        P(),
        P(("grp", "vid"), None),
        P(("grp", "vid")),
        P(("grp", "vid"), None),
        P(("grp", "vid"), None),
        P(("grp", "vid")),
    )
    return jax.shard_map(
        shards,
        mesh=mesh,
        in_specs=placed,
        out_specs=(P(("grp", "vid")), P(("grp", "vid"), None), P(("grp", "vid"), None)),
        check_vma=False,
    )
```

```python
import math

import jax
import jax.numpy as jnp
from jax import lax
from jax.experimental import pallas as pl
from jax.experimental.pallas import tpu as pltpu
from jax.sharding import PartitionSpec as P

F32 = jnp.float32
BF16 = jnp.bfloat16
HIDDEN = -1e30
EMBED_MIB = 52
TILES = 4
PIECES = 4
WIDE = 256
NT = (((1,), (1,)), ((), ()))
TN = (((0,), (0,)), ((), ()))
VMEM = pl.BlockSpec(memory_space=pltpu.VMEM)
SMEM = pl.BlockSpec(memory_space=pltpu.SMEM)
ANYWHERE = pl.BlockSpec(memory_space=pl.ANY)


def params(mib):
    return pltpu.CompilerParams(vmem_limit_bytes=mib * 2**20)


def cost(flops, nbytes, exps=0):
    return pl.CostEstimate(flops=flops, bytes_accessed=nbytes, transcendentals=exps)


def embed_kernel(x_hbm, w_hbm, e_ref, x_ref, w_ref, sem):
    tile = x_ref.shape[0] // TILES
    deep = w_ref.shape[0] // TILES
    reads = []
    for n in range(TILES):
        at = pl.ds(n * deep, deep)
        reads.append(pltpu.make_async_copy(w_hbm.at[at], w_ref.at[at], sem.at[n]))
    for n in range(TILES):
        at = pl.ds(n * tile, tile)
        reads.append(pltpu.make_async_copy(x_hbm.at[at], x_ref.at[at], sem.at[TILES + n]))
    for read in reads:
        read.start()
    for read in reads[:TILES]:
        read.wait()
    for n in range(TILES):
        reads[TILES + n].wait()
        at = slice(n * tile, (n + 1) * tile)
        e_ref[at, :] = jnp.dot(x_ref[at, :], w_ref[...], preferred_element_type=F32).astype(BF16)


def embed(frames, w):
    rows, depth = frames.shape
    width = w.shape[1]
    return pl.pallas_call(
        embed_kernel,
        in_specs=[ANYWHERE, ANYWHERE],
        out_specs=VMEM,
        out_shape=jax.ShapeDtypeStruct((rows, width), BF16),
        scratch_shapes=[
            pltpu.VMEM((rows, depth), BF16),
            pltpu.VMEM((depth, width), BF16),
            pltpu.SemaphoreType.DMA((2 * TILES,)),
        ],
        cost_estimate=cost(2 * rows * depth * width, 2 * (rows * depth + depth * width + rows * width)),
        compiler_params=params(EMBED_MIB),
        name="embed",
    )(frames, w)


def sight_kernel(place_ref, count_ref, tf_ref, ts_ref, keep_ref, give_ref):
    chips, rows = keep_ref.shape
    slots = tf_ref.shape[1]
    line = lax.broadcasted_iota(jnp.int32, (chips, slots), 0)
    slot = lax.broadcasted_iota(jnp.int32, (chips, slots), 1)
    block = lax.broadcasted_iota(jnp.int32, (rows, slots), 0) // 128
    right = jnp.where(tf_ref[...] == block, 1.0, 0.0).astype(BF16)
    for core, out_ref in enumerate((keep_ref, give_ref)):
        video = (2 * line + core) ^ place_ref[0]
        left = jnp.where((ts_ref[...] == video) & (slot < count_ref[0]), 1.0, 0.0).astype(BF16)
        seen = lax.dot_general(left, right, NT, preferred_element_type=F32)
        out_ref[...] = jnp.where(seen > 0.5, 0.0, HIDDEN)


def sight(place, count, tf, ts, chips, rows):
    return pl.pallas_call(
        sight_kernel,
        in_specs=[SMEM, SMEM, VMEM, VMEM],
        out_specs=[VMEM, VMEM],
        out_shape=[jax.ShapeDtypeStruct((chips, rows), F32)] * 2,
        compiler_params=params(24),
        name="sight",
    )(place, count, tf, ts)


def columns(rows):
    for half in range(2):
        for at in range(0, rows, WIDE):
            yield half, slice(at, at + WIDE), slice(half * rows + at, half * rows + at + WIDE)


def score_kernel(ks, temper, *refs):
    n = len(ks)
    es, biases = refs[:2], refs[2:4]
    blocks = refs[4 : 4 + n]
    refs = refs[4 + n :]
    if 0 in ks:
        goal_ref, st_in = refs[0], None
    else:
        st_in = refs[0]
    ps, top_ref, st_ref = refs[1 : 1 + n], refs[1 + n], refs[2 + n]
    rows, own = es[0].shape[0], blocks[0].shape[0]
    table = blocks[0][...] if n == 1 else jnp.concatenate([ref[...] for ref in blocks], axis=0)
    for half, at, to in columns(rows):
        s = lax.dot_general(table, es[half][at, :], NT, preferred_element_type=F32) * temper
        cuts = [s[m * own : (m + 1) * own] for m in range(n)]
        if 0 in ks and half == 0:
            hit = goal_ref[:, at] == lax.broadcasted_iota(jnp.int32, (own, WIDE), 0)
            found = jnp.sum(jnp.where(hit, cuts[ks.index(0)], 0.0), axis=0, keepdims=True)
            refs[3 + n][:, at] = found
        top = None if st_in is None else st_in[0:1, to]
        for m, k in enumerate(ks):
            cuts[m] = cuts[m] + biases[half][k : k + 1, at]
            high = jnp.max(cuts[m], axis=0, keepdims=True)
            top = high if top is None else jnp.maximum(top, high)
        total = None if st_in is None else st_in[1:2, to] * jnp.exp(st_in[0:1, to] - top)
        for m in range(n):
            p = jnp.exp(cuts[m] - top)
            ps[m][:, to] = p
            part = jnp.sum(p, axis=0, keepdims=True)
            total = part if total is None else total + part
        top_ref[:, to] = top
        st_ref[0:1, to] = top
        st_ref[1:2, to] = total


def score(ks, temper, es, biases, blocks, last):
    rows, width = es[0].shape
    own = blocks[0].shape[0]
    shapes = [jax.ShapeDtypeStruct((own, 2 * rows), F32)] * len(ks)
    shapes += [jax.ShapeDtypeStruct((1, 2 * rows), F32)]
    shapes += [jax.ShapeDtypeStruct((2, 2 * rows), F32)]
    shapes += [jax.ShapeDtypeStruct((1, rows), F32)] * (0 in ks)
    made = pl.pallas_call(
        lambda *refs: score_kernel(ks, temper, *refs),
        in_specs=[VMEM] * (5 + len(ks)),
        out_specs=[VMEM] * len(shapes),
        out_shape=shapes,
        cost_estimate=cost(
            4 * len(ks) * own * rows * width, 4 * rows * width + 8 * len(ks) * own * rows
        ),
        compiler_params=params(24),
        name=f"score_{ks[-1]}",
    )(*es, *biases, *blocks, last)
    return made[: len(ks)], made[len(ks)], made[len(ks) + 1 :]


def share_kernel(ks, *refs):
    st_ref, got_ref = refs[:2]
    es = refs[2:4]
    n = len(ks)
    ps, tops = refs[4 : 4 + n], refs[4 + n : 4 + 2 * n]
    refs = refs[4 + 2 * n :]
    if 0 in ks:
        goal_ref, pos_ref = refs[:2]
        refs = refs[2:]
    qs, outs = refs[:n], refs[n : 2 * n]
    rows = es[0].shape[0]
    for half in range(2):
        here = slice(half * rows, (half + 1) * rows)
        there = slice((1 - half) * rows, (2 - half) * rows)
        top, other = st_ref[0:1, here], got_ref[0:1, there]
        last = jnp.maximum(top, other)
        total = st_ref[1:2, here] * jnp.exp(top - last) + got_ref[1:2, there] * jnp.exp(other - last)
        if 0 in ks and half == 0:
            refs[2 * n][...] = last + jnp.log(total) - pos_ref[...]
        inverse = 1.0 / total
        for m, k in enumerate(ks):
            scale = jnp.exp(tops[m][:, here] - last) * inverse
            for at in range(0, rows, WIDE):
                to = slice(half * rows + at, half * rows + at + WIDE)
                q = (ps[m][:, to] * scale[:, at : at + WIDE]).astype(BF16)
                if k == 0 and half == 0:
                    hit = goal_ref[:, to] == lax.broadcasted_iota(jnp.int32, q.shape, 0)
                    q = (q.astype(F32) - jnp.where(hit, 1.0, 0.0)).astype(BF16)
                qs[m][:, to] = q
    for m in range(n):
        out = jnp.dot(qs[m][:, :rows], es[0][...], preferred_element_type=F32)
        out = out + jnp.dot(qs[m][:, rows:], es[1][...], preferred_element_type=F32)
        outs[m][...] = out.astype(outs[m].dtype)


def share(ks, kept, st, got, es, *more):
    own, rows2 = kept[ks[0]][0].shape
    width = es[0].shape[1]
    n = len(ks)
    shapes = [jax.ShapeDtypeStruct((own, rows2), BF16)] * n
    shapes += [jax.ShapeDtypeStruct((own, width), BF16 if k % 2 else F32) for k in ks]
    shapes += [jax.ShapeDtypeStruct((1, rows2 // 2), F32)] * (0 in ks)
    made = pl.pallas_call(
        lambda *refs: share_kernel(ks, *refs),
        in_specs=[VMEM] * (4 + 2 * n + len(more)),
        out_specs=[VMEM] * len(shapes),
        out_shape=shapes,
        cost_estimate=cost(2 * n * own * rows2 * width, n * 6 * own * rows2 + 2 * rows2 * width),
        compiler_params=params(40),
        name=f"share_{ks[0]}",
    )(st, got, *es, *[kept[k][0] for k in ks], *[kept[k][1] for k in ks], *more)
    return made[:n], made[n : 2 * n], made[2 * n :]


def part_rows(qs, table, at):
    q = jnp.concatenate([q_ref[:, at] for q_ref in qs], axis=0)
    return lax.dot_general(q, table, TN, preferred_element_type=F32)


def rows_kernel(n, first, *refs):
    table = jnp.concatenate([ref[...] for ref in refs[n : 2 * n]], axis=0)
    for turn, out_ref in enumerate(refs[2 * n :]):
        base = first + turn * out_ref.shape[0]
        for at in range(0, out_ref.shape[0], WIDE):
            part = part_rows(refs[:n], table, slice(base + at, base + at + WIDE))
            out_ref[at : at + WIDE, :] = part.astype(out_ref.dtype)


def rows_of(qs, blocks, theirs):
    n = len(qs)
    own, rows2 = qs[0].shape
    rows, width = rows2 // 2, blocks[0].shape[1]
    cut = PIECES if theirs else 1
    shape = jax.ShapeDtypeStruct((rows // cut, width), BF16 if theirs else F32)
    return pl.pallas_call(
        lambda *refs: rows_kernel(n, rows if theirs else 0, *refs),
        in_specs=[VMEM] * (2 * n),
        out_specs=[VMEM] * cut,
        out_shape=[shape] * cut,
        cost_estimate=cost(n * own * rows2 * width, 2 * n * own * (rows2 + width)),
        compiler_params=params(24),
        name="rows_theirs" if theirs else "rows_mine",
    )(*qs, *blocks)


def back_kernel(temper, mine_ref, w_ref, *refs):
    *gots, out_hbm, out_ref, sem = refs
    size = gots[0].shape[0]
    writes = []
    for turn, at in enumerate(range(0, out_ref.shape[0], WIDE)):
        cut = slice(at, at + WIDE)
        inner = slice(at % size, at % size + WIDE)
        g = (mine_ref[cut, :] + gots[at // size][inner, :].astype(F32)) * temper
        out_ref[cut, :] = lax.dot_general(
            g.astype(BF16), w_ref[...], NT, preferred_element_type=F32
        ).astype(BF16)
        cut = pl.ds(at, WIDE)
        writes.append(pltpu.make_async_copy(out_ref.at[cut], out_hbm.at[cut], sem.at[turn]))
        writes[-1].start()
    for write in writes:
        write.wait()


def back(mine, gots, w, temper):
    rows, width = mine.shape
    depth = w.shape[0]
    return pl.pallas_call(
        lambda *refs: back_kernel(temper, *refs),
        in_specs=[VMEM] * (2 + len(gots)),
        out_specs=ANYWHERE,
        out_shape=jax.ShapeDtypeStruct((rows, depth), BF16),
        scratch_shapes=[
            pltpu.VMEM((rows, depth), BF16),
            pltpu.SemaphoreType.DMA((rows // WIDE,)),
        ],
        cost_estimate=cost(2 * rows * width * depth, 2 * (depth * width + rows * depth)),
        compiler_params=params(40),
        name="back",
    )(mine, w, *gots)


def finish_kernel(temper, *refs):
    own_ref, *come_refs, out_hbm, out_ref, sem = refs
    tile = out_ref.shape[0] // TILES
    writes = []
    for n in range(TILES):
        at = slice(n * tile, (n + 1) * tile)
        total = own_ref[at, :]
        for come_ref in come_refs:
            total = total + come_ref[at, :].astype(F32)
        out_ref[at, :] = total * temper
        cut = pl.ds(n * tile, tile)
        writes.append(pltpu.make_async_copy(out_ref.at[cut], out_hbm.at[cut], sem.at[n]))
        writes[n].start()
    for write in writes:
        write.wait()


def finish(own, come, temper):
    return pl.pallas_call(
        lambda *refs: finish_kernel(temper, *refs),
        in_specs=[VMEM] * (1 + len(come)),
        out_specs=ANYWHERE,
        out_shape=jax.ShapeDtypeStruct(own.shape, F32),
        scratch_shapes=[pltpu.VMEM(own.shape, F32), pltpu.SemaphoreType.DMA((TILES,))],
        compiler_params=params(24),
        name="finish",
    )(own, *come)


def shards(frames, w_frame, step_emb, targets, tile_frame, tile_step, tile_count):
    videos = lax.axis_size("vid")
    chips = videos // 2
    rows = frames.shape[0]
    temper = 1.0 / math.sqrt(step_emb.shape[1])
    place = lax.axis_index("vid").astype(jnp.int32).reshape(1)
    goals = targets.reshape(1, -1)

    def trade(x, k):
        return lax.ppermute(x, "vid", [(i, i ^ k) for i in range(videos)])

    order, bit = [0], chips // 2
    while bit:
        order += [k ^ bit for k in order]
        bit //= 2
    e = embed(frames, w_frame)
    keep, lend = sight(place, tile_count, tile_frame, tile_step, chips, rows)
    biases = (keep, trade(lend, 1))
    mine, kept, st = {0: step_emb}, {}, goals
    near = trade(step_emb, 2)
    far = chips // 2
    come = trade(step_emb, 2 * far)
    mine[1], mine[far], e = lax.optimization_barrier((near, come, e))
    es = (e, trade(e, 1))
    early = (0, far, 1)
    for ks in [early] + [(k,) for k in order if k not in early]:
        k = ks[0]
        if k > 0:
            low = k & -k
            come = trade(mine[k ^ low], 2 * low)
            mine[k], gate = lax.optimization_barrier((come, st))
        ps, top, (st, *pos) = score(ks, temper, es, biases, [mine[m] for m in ks], st)
        if pos:
            found = pos[0]
        for m, p in zip(ks, ps):
            kept[m] = (p, top)
    got = trade(st, 1)

    qs, sums = {}, {}
    for ks in [(k,) for k in range(chips - 1, 2, -1)] + [(2, 1, 0)]:
        more = (goals, found) if 0 in ks else ()
        made, parts, loss = share(ks, kept, st, got, es, *more)
        qs.update(zip(ks, made))
        sums.update(zip(ks, parts))
        if 0 not in ks:
            e, qs[ks[0]] = lax.optimization_barrier((es[0], qs[ks[0]]))
            es = (e, es[1])
    parts = [qs[k] for k in order], [mine[k] for k in order]
    lent = [trade(piece, 1) for piece in rows_of(*parts, True)]
    (own_rows,) = rows_of(*parts, False)
    frame_grad = back(own_rows, lent, w_frame, temper)
    bit, ends = 1, []
    while bit < chips:
        for k in range(chips - bit, 0, -2 * bit):
            come = trade(sums[k].astype(BF16), 2 * bit)
            if k == bit:
                ends.append(come)
            else:
                sums[k - bit] = sums[k - bit].astype(F32) + come.astype(F32)
        bit *= 2
    *ends, frame_grad = lax.optimization_barrier((*ends, frame_grad))
    step_grad = finish(sums[0], ends, temper)
    return (loss[0].reshape(-1), frame_grad, step_grad)


def solution(mesh):
    placed = (
        P(("grp", "vid"), None),
        P(),
        P(("grp", "vid"), None),
        P(("grp", "vid")),
        P(("grp", "vid"), None),
        P(("grp", "vid"), None),
        P(("grp", "vid")),
    )
    return jax.shard_map(
        shards,
        mesh=mesh,
        in_specs=placed,
        out_specs=(P(("grp", "vid")), P(("grp", "vid"), None), P(("grp", "vid"), None)),
        check_vma=False,
    )
```

```python
import math

import jax
import jax.numpy as jnp
from jax import lax
from jax.experimental import pallas as pl
from jax.experimental.pallas import tpu as pltpu
from jax.sharding import PartitionSpec as P

F32 = jnp.float32
BF16 = jnp.bfloat16
HIDDEN = -1e30
EMBED_MIB = 52
TILES = 4
PIECES = 4
WIDE = 256
SPAN = 512
NT = (((1,), (1,)), ((), ()))
TN = (((0,), (0,)), ((), ()))
VMEM = pl.BlockSpec(memory_space=pltpu.VMEM)
SMEM = pl.BlockSpec(memory_space=pltpu.SMEM)
ANYWHERE = pl.BlockSpec(memory_space=pl.ANY)


def params(mib):
    return pltpu.CompilerParams(vmem_limit_bytes=mib * 2**20)


def cost(flops, nbytes, exps=0):
    return pl.CostEstimate(flops=flops, bytes_accessed=nbytes, transcendentals=exps)


def embed_kernel(x_hbm, w_hbm, e_ref, x_ref, w_ref, sem):
    tile = x_ref.shape[0] // TILES
    deep = w_ref.shape[0] // TILES
    reads = []
    for n in range(TILES):
        at = pl.ds(n * deep, deep)
        reads.append(pltpu.make_async_copy(w_hbm.at[at], w_ref.at[at], sem.at[n]))
    for n in range(TILES):
        at = pl.ds(n * tile, tile)
        reads.append(pltpu.make_async_copy(x_hbm.at[at], x_ref.at[at], sem.at[TILES + n]))
    for read in reads:
        read.start()
    for read in reads[:TILES]:
        read.wait()
    for n in range(TILES):
        reads[TILES + n].wait()
        at = slice(n * tile, (n + 1) * tile)
        e_ref[at, :] = jnp.dot(x_ref[at, :], w_ref[...], preferred_element_type=F32).astype(BF16)


def embed(frames, w):
    rows, depth = frames.shape
    width = w.shape[1]
    return pl.pallas_call(
        embed_kernel,
        in_specs=[ANYWHERE, ANYWHERE],
        out_specs=VMEM,
        out_shape=jax.ShapeDtypeStruct((rows, width), BF16),
        scratch_shapes=[
            pltpu.VMEM((rows, depth), BF16),
            pltpu.VMEM((depth, width), BF16),
            pltpu.SemaphoreType.DMA((2 * TILES,)),
        ],
        cost_estimate=cost(2 * rows * depth * width, 2 * (rows * depth + depth * width + rows * width)),
        compiler_params=params(EMBED_MIB),
        name="embed",
    )(frames, w)


def sight_kernel(place_ref, count_ref, tf_ref, ts_ref, keep_ref, give_ref):
    chips, rows = keep_ref.shape
    slots = tf_ref.shape[1]
    line = lax.broadcasted_iota(jnp.int32, (chips, slots), 0)
    slot = lax.broadcasted_iota(jnp.int32, (chips, slots), 1)
    block = lax.broadcasted_iota(jnp.int32, (rows, slots), 0) // 128
    right = jnp.where(tf_ref[...] == block, 1.0, 0.0).astype(BF16)
    for core, out_ref in enumerate((keep_ref, give_ref)):
        video = (2 * line + core) ^ place_ref[0]
        left = jnp.where((ts_ref[...] == video) & (slot < count_ref[0]), 1.0, 0.0).astype(BF16)
        seen = lax.dot_general(left, right, NT, preferred_element_type=F32)
        out_ref[...] = jnp.where(seen > 0.5, 0.0, HIDDEN)


def sight(place, count, tf, ts, chips, rows):
    return pl.pallas_call(
        sight_kernel,
        in_specs=[SMEM, SMEM, VMEM, VMEM],
        out_specs=[VMEM, VMEM],
        out_shape=[jax.ShapeDtypeStruct((chips, rows), F32)] * 2,
        compiler_params=params(24),
        name="sight",
    )(place, count, tf, ts)


def columns(rows):
    for half in range(2):
        for at in range(0, rows, SPAN):
            yield half, slice(at, at + SPAN), slice(half * rows + at, half * rows + at + SPAN)


def score_kernel(ks, temper, *refs):
    n = len(ks)
    es, biases = refs[:2], refs[2:4]
    blocks = refs[4 : 4 + n]
    refs = refs[4 + n :]
    if 0 in ks:
        goal_ref, st_in = refs[0], None
    else:
        st_in = refs[0]
    ps, top_ref, st_ref = refs[1 : 1 + n], refs[1 + n], refs[2 + n]
    rows, own = es[0].shape[0], blocks[0].shape[0]
    table = blocks[0][...] if n == 1 else jnp.concatenate([ref[...] for ref in blocks], axis=0)
    for half, at, to in columns(rows):
        s = lax.dot_general(table, es[half][at, :], NT, preferred_element_type=F32) * temper
        cuts = [s[m * own : (m + 1) * own] for m in range(n)]
        if 0 in ks and half == 0:
            hit = goal_ref[:, at] == lax.broadcasted_iota(jnp.int32, (own, SPAN), 0)
            found = jnp.sum(jnp.where(hit, cuts[ks.index(0)], 0.0), axis=0, keepdims=True)
            refs[3 + n][:, at] = found
        top = None if st_in is None else st_in[0:1, to]
        for m, k in enumerate(ks):
            cuts[m] = cuts[m] + biases[half][k : k + 1, at]
            high = jnp.max(cuts[m], axis=0, keepdims=True)
            top = high if top is None else jnp.maximum(top, high)
        total = None if st_in is None else st_in[1:2, to] * jnp.exp(st_in[0:1, to] - top)
        for m in range(n):
            p = jnp.exp(cuts[m] - top)
            ps[m][:, to] = p
            part = jnp.sum(p, axis=0, keepdims=True)
            total = part if total is None else total + part
        top_ref[:, to] = top
        st_ref[0:1, to] = top
        st_ref[1:2, to] = total


def score(ks, temper, es, biases, blocks, last):
    rows, width = es[0].shape
    own = blocks[0].shape[0]
    shapes = [jax.ShapeDtypeStruct((own, 2 * rows), F32)] * len(ks)
    shapes += [jax.ShapeDtypeStruct((1, 2 * rows), F32)]
    shapes += [jax.ShapeDtypeStruct((2, 2 * rows), F32)]
    shapes += [jax.ShapeDtypeStruct((1, rows), F32)] * (0 in ks)
    made = pl.pallas_call(
        lambda *refs: score_kernel(ks, temper, *refs),
        in_specs=[VMEM] * (5 + len(ks)),
        out_specs=[VMEM] * len(shapes),
        out_shape=shapes,
        cost_estimate=cost(
            4 * len(ks) * own * rows * width, 4 * rows * width + 8 * len(ks) * own * rows
        ),
        compiler_params=params(24),
        name=f"score_{ks[-1]}",
    )(*es, *biases, *blocks, last)
    return made[: len(ks)], made[len(ks)], made[len(ks) + 1 :]


def share_kernel(ks, *refs):
    st_ref, got_ref = refs[:2]
    es = refs[2:4]
    n = len(ks)
    ps, tops = refs[4 : 4 + n], refs[4 + n : 4 + 2 * n]
    refs = refs[4 + 2 * n :]
    if 0 in ks:
        goal_ref, pos_ref = refs[:2]
        refs = refs[2:]
    qs, outs = refs[:n], refs[n : 2 * n]
    rows = es[0].shape[0]
    for half in range(2):
        here = slice(half * rows, (half + 1) * rows)
        there = slice((1 - half) * rows, (2 - half) * rows)
        top, other = st_ref[0:1, here], got_ref[0:1, there]
        last = jnp.maximum(top, other)
        total = st_ref[1:2, here] * jnp.exp(top - last) + got_ref[1:2, there] * jnp.exp(other - last)
        if 0 in ks and half == 0:
            refs[2 * n][...] = last + jnp.log(total) - pos_ref[...]
        inverse = 1.0 / total
        for m, k in enumerate(ks):
            scale = jnp.exp(tops[m][:, here] - last) * inverse
            for at in range(0, rows, WIDE):
                to = slice(half * rows + at, half * rows + at + WIDE)
                q = (ps[m][:, to] * scale[:, at : at + WIDE]).astype(BF16)
                if k == 0 and half == 0:
                    hit = goal_ref[:, to] == lax.broadcasted_iota(jnp.int32, q.shape, 0)
                    q = (q.astype(F32) - jnp.where(hit, 1.0, 0.0)).astype(BF16)
                qs[m][:, to] = q
    for m in range(n):
        out = jnp.dot(qs[m][:, :rows], es[0][...], preferred_element_type=F32)
        out = out + jnp.dot(qs[m][:, rows:], es[1][...], preferred_element_type=F32)
        outs[m][...] = out.astype(outs[m].dtype)


def share(ks, kept, st, got, es, *more):
    own, rows2 = kept[ks[0]][0].shape
    width = es[0].shape[1]
    n = len(ks)
    shapes = [jax.ShapeDtypeStruct((own, rows2), BF16)] * n
    shapes += [jax.ShapeDtypeStruct((own, width), BF16 if k % 2 else F32) for k in ks]
    shapes += [jax.ShapeDtypeStruct((1, rows2 // 2), F32)] * (0 in ks)
    made = pl.pallas_call(
        lambda *refs: share_kernel(ks, *refs),
        in_specs=[VMEM] * (4 + 2 * n + len(more)),
        out_specs=[VMEM] * len(shapes),
        out_shape=shapes,
        cost_estimate=cost(2 * n * own * rows2 * width, n * 6 * own * rows2 + 2 * rows2 * width),
        compiler_params=params(40),
        name=f"share_{ks[0]}",
    )(st, got, *es, *[kept[k][0] for k in ks], *[kept[k][1] for k in ks], *more)
    return made[:n], made[n : 2 * n], made[2 * n :]


def part_rows(qs, table, at):
    q = jnp.concatenate([q_ref[:, at] for q_ref in qs], axis=0)
    return lax.dot_general(q, table, TN, preferred_element_type=F32)


def rows_kernel(n, first, *refs):
    table = jnp.concatenate([ref[...] for ref in refs[n : 2 * n]], axis=0)
    for turn, out_ref in enumerate(refs[2 * n :]):
        base = first + turn * out_ref.shape[0]
        for at in range(0, out_ref.shape[0], WIDE):
            part = part_rows(refs[:n], table, slice(base + at, base + at + WIDE))
            out_ref[at : at + WIDE, :] = part.astype(out_ref.dtype)


def rows_of(qs, blocks, theirs):
    n = len(qs)
    own, rows2 = qs[0].shape
    rows, width = rows2 // 2, blocks[0].shape[1]
    cut = PIECES if theirs else 1
    shape = jax.ShapeDtypeStruct((rows // cut, width), BF16 if theirs else F32)
    return pl.pallas_call(
        lambda *refs: rows_kernel(n, rows if theirs else 0, *refs),
        in_specs=[VMEM] * (2 * n),
        out_specs=[VMEM] * cut,
        out_shape=[shape] * cut,
        cost_estimate=cost(n * own * rows2 * width, 2 * n * own * (rows2 + width)),
        compiler_params=params(24),
        name="rows_theirs" if theirs else "rows_mine",
    )(*qs, *blocks)


def back_kernel(temper, mine_ref, w_ref, *refs):
    *gots, out_hbm, out_ref, sem = refs
    size = gots[0].shape[0]
    writes = []
    for turn, at in enumerate(range(0, out_ref.shape[0], WIDE)):
        cut = slice(at, at + WIDE)
        inner = slice(at % size, at % size + WIDE)
        g = (mine_ref[cut, :] + gots[at // size][inner, :].astype(F32)) * temper
        out_ref[cut, :] = lax.dot_general(
            g.astype(BF16), w_ref[...], NT, preferred_element_type=F32
        ).astype(BF16)
        cut = pl.ds(at, WIDE)
        writes.append(pltpu.make_async_copy(out_ref.at[cut], out_hbm.at[cut], sem.at[turn]))
        writes[-1].start()
    for write in writes:
        write.wait()


def back(mine, gots, w, temper):
    rows, width = mine.shape
    depth = w.shape[0]
    return pl.pallas_call(
        lambda *refs: back_kernel(temper, *refs),
        in_specs=[VMEM] * (2 + len(gots)),
        out_specs=ANYWHERE,
        out_shape=jax.ShapeDtypeStruct((rows, depth), BF16),
        scratch_shapes=[
            pltpu.VMEM((rows, depth), BF16),
            pltpu.SemaphoreType.DMA((rows // WIDE,)),
        ],
        cost_estimate=cost(2 * rows * width * depth, 2 * (depth * width + rows * depth)),
        compiler_params=params(40),
        name="back",
    )(mine, w, *gots)


def shards(frames, w_frame, step_emb, targets, tile_frame, tile_step, tile_count):
    videos = lax.axis_size("vid")
    chips = videos // 2
    rows = frames.shape[0]
    temper = 1.0 / math.sqrt(step_emb.shape[1])
    place = lax.axis_index("vid").astype(jnp.int32).reshape(1)
    goals = targets.reshape(1, -1)

    def trade(x, k):
        return lax.ppermute(x, "vid", [(i, i ^ k) for i in range(videos)])

    order, bit = [0], chips // 2
    while bit:
        order += [k ^ bit for k in order]
        bit //= 2
    e = embed(frames, w_frame)
    keep, lend = sight(place, tile_count, tile_frame, tile_step, chips, rows)
    biases = (keep, trade(lend, 1))
    mine, kept, st = {0: step_emb}, {}, goals
    near = trade(step_emb, 2)
    far = chips // 2
    come = trade(step_emb, 2 * far)
    mine[1], mine[far], e = lax.optimization_barrier((near, come, e))
    es = (e, trade(e, 1))
    early = (0, far, 1)
    for ks in [early] + [(k,) for k in order if k not in early]:
        k = ks[0]
        if k > 0:
            low = k & -k
            come = trade(mine[k ^ low], 2 * low)
            mine[k], gate = lax.optimization_barrier((come, st))
        ps, top, (st, *pos) = score(ks, temper, es, biases, [mine[m] for m in ks], st)
        if pos:
            found = pos[0]
        for m, p in zip(ks, ps):
            kept[m] = (p, top)
    got = trade(st, 1)

    qs, sums = {}, {}
    for ks in [(k,) for k in range(chips - 1, 2, -1)] + [(2, 1, 0)]:
        more = (goals, found) if 0 in ks else ()
        made, parts, loss = share(ks, kept, st, got, es, *more)
        qs.update(zip(ks, made))
        sums.update(zip(ks, parts))
        if 0 not in ks:
            e, qs[ks[0]] = lax.optimization_barrier((es[0], qs[ks[0]]))
            es = (e, es[1])
    parts = [qs[k] for k in order], [mine[k] for k in order]
    lent = [trade(piece, 1) for piece in rows_of(*parts, True)]
    (own_rows,) = rows_of(*parts, False)
    frame_grad = back(own_rows, lent, w_frame, temper)
    bit = 1
    while bit < chips:
        for k in range(chips - bit, 0, -2 * bit):
            come = trade(sums[k].astype(BF16), 2 * bit)
            if 2 * bit == chips:
                come, frame_grad = lax.optimization_barrier((come, frame_grad))
            sums[k - bit] = sums[k - bit].astype(F32) + come.astype(F32)
        bit *= 2
    return (loss[0].reshape(-1), frame_grad, sums[0] * temper)


def solution(mesh):
    placed = (
        P(("grp", "vid"), None),
        P(),
        P(("grp", "vid"), None),
        P(("grp", "vid")),
        P(("grp", "vid"), None),
        P(("grp", "vid"), None),
        P(("grp", "vid")),
    )
    return jax.shard_map(
        shards,
        mesh=mesh,
        in_specs=placed,
        out_specs=(P(("grp", "vid")), P(("grp", "vid"), None), P(("grp", "vid"), None)),
        check_vma=False,
    )
```

```python
import math

import jax
import jax.numpy as jnp
from jax import lax
from jax.experimental import pallas as pl
from jax.experimental.pallas import tpu as pltpu
from jax.sharding import PartitionSpec as P

F32 = jnp.float32
BF16 = jnp.bfloat16
HIDDEN = -1e30
EMBED_MIB = 52
TILES = 4
PIECES = 4
WIDE = 256
NT = (((1,), (1,)), ((), ()))
TN = (((0,), (0,)), ((), ()))
VMEM = pl.BlockSpec(memory_space=pltpu.VMEM)
SMEM = pl.BlockSpec(memory_space=pltpu.SMEM)
ANYWHERE = pl.BlockSpec(memory_space=pl.ANY)


def params(mib):
    return pltpu.CompilerParams(vmem_limit_bytes=mib * 2**20)


def cost(flops, nbytes, exps=0):
    return pl.CostEstimate(flops=flops, bytes_accessed=nbytes, transcendentals=exps)


def embed_kernel(x_hbm, w_hbm, e_ref, x_ref, w_ref, sem):
    tile = x_ref.shape[0] // TILES
    deep = w_ref.shape[0] // TILES
    reads = []
    for n in range(TILES):
        at = pl.ds(n * deep, deep)
        reads.append(pltpu.make_async_copy(w_hbm.at[at], w_ref.at[at], sem.at[n]))
    for n in range(TILES):
        at = pl.ds(n * tile, tile)
        reads.append(pltpu.make_async_copy(x_hbm.at[at], x_ref.at[at], sem.at[TILES + n]))
    for read in reads:
        read.start()
    for read in reads[:TILES]:
        read.wait()
    for n in range(TILES):
        reads[TILES + n].wait()
        at = slice(n * tile, (n + 1) * tile)
        e_ref[at, :] = jnp.dot(x_ref[at, :], w_ref[...], preferred_element_type=F32).astype(BF16)


def embed(frames, w):
    rows, depth = frames.shape
    width = w.shape[1]
    return pl.pallas_call(
        embed_kernel,
        in_specs=[ANYWHERE, ANYWHERE],
        out_specs=VMEM,
        out_shape=jax.ShapeDtypeStruct((rows, width), BF16),
        scratch_shapes=[
            pltpu.VMEM((rows, depth), BF16),
            pltpu.VMEM((depth, width), BF16),
            pltpu.SemaphoreType.DMA((2 * TILES,)),
        ],
        cost_estimate=cost(2 * rows * depth * width, 2 * (rows * depth + depth * width + rows * width)),
        compiler_params=params(EMBED_MIB),
        name="embed",
    )(frames, w)


def sight_kernel(place_ref, count_ref, tf_ref, ts_ref, keep_ref, give_ref):
    chips, rows = keep_ref.shape
    slots = tf_ref.shape[1]
    line = lax.broadcasted_iota(jnp.int32, (chips, slots), 0)
    slot = lax.broadcasted_iota(jnp.int32, (chips, slots), 1)
    block = lax.broadcasted_iota(jnp.int32, (rows, slots), 0) // 128
    right = jnp.where(tf_ref[...] == block, 1.0, 0.0).astype(BF16)
    for core, out_ref in enumerate((keep_ref, give_ref)):
        video = (2 * line + core) ^ place_ref[0]
        left = jnp.where((ts_ref[...] == video) & (slot < count_ref[0]), 1.0, 0.0).astype(BF16)
        seen = lax.dot_general(left, right, NT, preferred_element_type=F32)
        out_ref[...] = jnp.where(seen > 0.5, 0.0, HIDDEN)


def sight(place, count, tf, ts, chips, rows):
    return pl.pallas_call(
        sight_kernel,
        in_specs=[SMEM, SMEM, VMEM, VMEM],
        out_specs=[VMEM, VMEM],
        out_shape=[jax.ShapeDtypeStruct((chips, rows), F32)] * 2,
        compiler_params=params(24),
        name="sight",
    )(place, count, tf, ts)


def columns(rows):
    for half in range(2):
        for at in range(0, rows, WIDE):
            yield half, slice(at, at + WIDE), slice(half * rows + at, half * rows + at + WIDE)


def score_kernel(ks, temper, *refs):
    n = len(ks)
    es, biases = refs[:2], refs[2:4]
    blocks = refs[4 : 4 + n]
    refs = refs[4 + n :]
    if 0 in ks:
        goal_ref, st_in = refs[0], None
    else:
        st_in = refs[0]
    ps, top_ref, st_ref = refs[1 : 1 + n], refs[1 + n], refs[2 + n]
    rows, own = es[0].shape[0], blocks[0].shape[0]
    table = blocks[0][...] if n == 1 else jnp.concatenate([ref[...] for ref in blocks], axis=0)
    for half, at, to in columns(rows):
        s = lax.dot_general(table, es[half][at, :], NT, preferred_element_type=F32) * temper
        cuts = [s[m * own : (m + 1) * own] for m in range(n)]
        if 0 in ks and half == 0:
            hit = goal_ref[:, at] == lax.broadcasted_iota(jnp.int32, (own, WIDE), 0)
            found = jnp.sum(jnp.where(hit, cuts[ks.index(0)], 0.0), axis=0, keepdims=True)
            refs[3 + n][:, at] = found
        top = None if st_in is None else st_in[0:1, to]
        for m, k in enumerate(ks):
            cuts[m] = cuts[m] + biases[half][k : k + 1, at]
            high = jnp.max(cuts[m], axis=0, keepdims=True)
            top = high if top is None else jnp.maximum(top, high)
        total = None if st_in is None else st_in[1:2, to] * jnp.exp(st_in[0:1, to] - top)
        for m in range(n):
            p = jnp.exp(cuts[m] - top)
            ps[m][:, to] = p
            part = jnp.sum(p, axis=0, keepdims=True)
            total = part if total is None else total + part
        top_ref[:, to] = top
        st_ref[0:1, to] = top
        st_ref[1:2, to] = total


def score(ks, temper, es, biases, blocks, last):
    rows, width = es[0].shape
    own = blocks[0].shape[0]
    shapes = [jax.ShapeDtypeStruct((own, 2 * rows), F32)] * len(ks)
    shapes += [jax.ShapeDtypeStruct((1, 2 * rows), F32)]
    shapes += [jax.ShapeDtypeStruct((2, 2 * rows), F32)]
    shapes += [jax.ShapeDtypeStruct((1, rows), F32)] * (0 in ks)
    made = pl.pallas_call(
        lambda *refs: score_kernel(ks, temper, *refs),
        in_specs=[VMEM] * (5 + len(ks)),
        out_specs=[VMEM] * len(shapes),
        out_shape=shapes,
        cost_estimate=cost(
            4 * len(ks) * own * rows * width, 4 * rows * width + 8 * len(ks) * own * rows
        ),
        compiler_params=params(24),
        name=f"score_{ks[-1]}",
    )(*es, *biases, *blocks, last)
    return made[: len(ks)], made[len(ks)], made[len(ks) + 1 :]


def share_kernel(ks, *refs):
    st_ref, got_ref = refs[:2]
    es = refs[2:4]
    n = len(ks)
    ps, tops = refs[4 : 4 + n], refs[4 + n : 4 + 2 * n]
    refs = refs[4 + 2 * n :]
    if 0 in ks:
        goal_ref, pos_ref = refs[:2]
        refs = refs[2:]
    qs, outs = refs[:n], refs[n : 2 * n]
    rows = es[0].shape[0]
    for half in range(2):
        here = slice(half * rows, (half + 1) * rows)
        there = slice((1 - half) * rows, (2 - half) * rows)
        top, other = st_ref[0:1, here], got_ref[0:1, there]
        last = jnp.maximum(top, other)
        total = st_ref[1:2, here] * jnp.exp(top - last) + got_ref[1:2, there] * jnp.exp(other - last)
        if 0 in ks and half == 0:
            refs[2 * n][...] = last + jnp.log(total) - pos_ref[...]
        inverse = 1.0 / total
        for m, k in enumerate(ks):
            scale = jnp.exp(tops[m][:, here] - last) * inverse
            for at in range(0, rows, WIDE):
                to = slice(half * rows + at, half * rows + at + WIDE)
                q = (ps[m][:, to] * scale[:, at : at + WIDE]).astype(BF16)
                if k == 0 and half == 0:
                    hit = goal_ref[:, to] == lax.broadcasted_iota(jnp.int32, q.shape, 0)
                    q = (q.astype(F32) - jnp.where(hit, 1.0, 0.0)).astype(BF16)
                qs[m][:, to] = q
    for m in range(n):
        out = jnp.dot(qs[m][:, :rows], es[0][...], preferred_element_type=F32)
        out = out + jnp.dot(qs[m][:, rows:], es[1][...], preferred_element_type=F32)
        outs[m][...] = out.astype(outs[m].dtype)


def share(ks, kept, st, got, es, *more):
    own, rows2 = kept[ks[0]][0].shape
    width = es[0].shape[1]
    n = len(ks)
    shapes = [jax.ShapeDtypeStruct((own, rows2), BF16)] * n
    shapes += [jax.ShapeDtypeStruct((own, width), BF16 if k % 2 else F32) for k in ks]
    shapes += [jax.ShapeDtypeStruct((1, rows2 // 2), F32)] * (0 in ks)
    made = pl.pallas_call(
        lambda *refs: share_kernel(ks, *refs),
        in_specs=[VMEM] * (4 + 2 * n + len(more)),
        out_specs=[VMEM] * len(shapes),
        out_shape=shapes,
        cost_estimate=cost(2 * n * own * rows2 * width, n * 6 * own * rows2 + 2 * rows2 * width),
        compiler_params=params(40),
        name=f"share_{ks[0]}",
    )(st, got, *es, *[kept[k][0] for k in ks], *[kept[k][1] for k in ks], *more)
    return made[:n], made[n : 2 * n], made[2 * n :]


def part_rows(qs, table, at):
    q = jnp.concatenate([q_ref[:, at] for q_ref in qs], axis=0)
    return lax.dot_general(q, table, TN, preferred_element_type=F32)


def rows_kernel(n, first, *refs):
    table = jnp.concatenate([ref[...] for ref in refs[n : 2 * n]], axis=0)
    for turn, out_ref in enumerate(refs[2 * n :]):
        base = first + turn * out_ref.shape[0]
        for at in range(0, out_ref.shape[0], WIDE):
            part = part_rows(refs[:n], table, slice(base + at, base + at + WIDE))
            out_ref[at : at + WIDE, :] = part.astype(out_ref.dtype)


def rows_of(qs, blocks, theirs):
    n = len(qs)
    own, rows2 = qs[0].shape
    rows, width = rows2 // 2, blocks[0].shape[1]
    cut = PIECES if theirs else 1
    shape = jax.ShapeDtypeStruct((rows // cut, width), BF16 if theirs else F32)
    return pl.pallas_call(
        lambda *refs: rows_kernel(n, rows if theirs else 0, *refs),
        in_specs=[VMEM] * (2 * n),
        out_specs=[VMEM] * cut,
        out_shape=[shape] * cut,
        cost_estimate=cost(n * own * rows2 * width, 2 * n * own * (rows2 + width)),
        compiler_params=params(24),
        name="rows_theirs" if theirs else "rows_mine",
    )(*qs, *blocks)


def back_kernel(temper, mine_ref, w_ref, *refs):
    *gots, out_hbm, out_ref, sem = refs
    size = gots[0].shape[0]
    writes = []
    for turn, at in enumerate(range(0, out_ref.shape[0], WIDE)):
        cut = slice(at, at + WIDE)
        inner = slice(at % size, at % size + WIDE)
        g = (mine_ref[cut, :] + gots[at // size][inner, :].astype(F32)) * temper
        out_ref[cut, :] = lax.dot_general(
            g.astype(BF16), w_ref[...], NT, preferred_element_type=F32
        ).astype(BF16)
        cut = pl.ds(at, WIDE)
        writes.append(pltpu.make_async_copy(out_ref.at[cut], out_hbm.at[cut], sem.at[turn]))
        writes[-1].start()
    for write in writes:
        write.wait()


def back(mine, gots, w, temper):
    rows, width = mine.shape
    depth = w.shape[0]
    return pl.pallas_call(
        lambda *refs: back_kernel(temper, *refs),
        in_specs=[VMEM] * (2 + len(gots)),
        out_specs=ANYWHERE,
        out_shape=jax.ShapeDtypeStruct((rows, depth), BF16),
        scratch_shapes=[
            pltpu.VMEM((rows, depth), BF16),
            pltpu.SemaphoreType.DMA((rows // WIDE,)),
        ],
        cost_estimate=cost(2 * rows * width * depth, 2 * (depth * width + rows * depth)),
        compiler_params=params(40),
        name="back",
    )(mine, w, *gots)


def shards(frames, w_frame, step_emb, targets, tile_frame, tile_step, tile_count):
    videos = lax.axis_size("vid")
    chips = videos // 2
    rows = frames.shape[0]
    temper = 1.0 / math.sqrt(step_emb.shape[1])
    place = lax.axis_index("vid").astype(jnp.int32).reshape(1)
    goals = targets.reshape(1, -1)

    def trade(x, k):
        return lax.ppermute(x, "vid", [(i, i ^ k) for i in range(videos)])

    order, bit = [0], chips // 2
    while bit:
        order += [k ^ bit for k in order]
        bit //= 2
    e = embed(frames, w_frame)
    keep, lend = sight(place, tile_count, tile_frame, tile_step, chips, rows)
    biases = (keep, trade(lend, 1))
    mine, kept, st = {0: step_emb}, {}, goals
    near = trade(step_emb, 2)
    far = chips // 2
    come = trade(step_emb, 2 * far)
    mine[1], mine[far], e = lax.optimization_barrier((near, come, e))
    es = (e, trade(e, 1))
    early = (0, far, 1)
    for ks in [early] + [(k,) for k in order if k not in early]:
        k = ks[0]
        if k > 0:
            low = k & -k
            come = trade(mine[k ^ low], 2 * low)
            mine[k], gate = lax.optimization_barrier((come, st))
        ps, top, (st, *pos) = score(ks, temper, es, biases, [mine[m] for m in ks], st)
        if pos:
            found = pos[0]
        for m, p in zip(ks, ps):
            kept[m] = (p, top)
    got = trade(st, 1)

    qs, sums = {}, {}
    for ks in [(k,) for k in range(chips - 1, 2, -1)] + [(2, 1, 0)]:
        more = (goals, found) if 0 in ks else ()
        made, parts, loss = share(ks, kept, st, got, es, *more)
        qs.update(zip(ks, made))
        sums.update(zip(ks, parts))
        if 0 not in ks:
            e, qs[ks[0]] = lax.optimization_barrier((es[0], qs[ks[0]]))
            es = (e, es[1])
    parts = [qs[k] for k in order], [mine[k] for k in order]
    lent = [trade(piece, 1) for piece in rows_of(*parts, True)]
    (own_rows,) = rows_of(*parts, False)
    sums[1], lent[0] = lax.optimization_barrier((sums[1], lent[0]))
    frame_grad = back(own_rows, lent, w_frame, temper)
    bit = 1
    while bit < chips:
        for k in range(chips - bit, 0, -2 * bit):
            come = trade(sums[k].astype(BF16), 2 * bit)
            if 2 * bit == chips:
                come, frame_grad = lax.optimization_barrier((come, frame_grad))
            sums[k - bit] = sums[k - bit].astype(F32) + come.astype(F32)
        bit *= 2
    return (loss[0].reshape(-1), frame_grad, sums[0] * temper)


def solution(mesh):
    placed = (
        P(("grp", "vid"), None),
        P(),
        P(("grp", "vid"), None),
        P(("grp", "vid")),
        P(("grp", "vid"), None),
        P(("grp", "vid"), None),
        P(("grp", "vid")),
    )
    return jax.shard_map(
        shards,
        mesh=mesh,
        in_specs=placed,
        out_specs=(P(("grp", "vid")), P(("grp", "vid"), None), P(("grp", "vid"), None)),
        check_vma=False,
    )
```
